32 devices in a mesh: row: 4 (over z), col: 8 (over y, x, core).
Axes of the slice: x: 2, y: 2, z: 4, core: 2. Of those that a mesh axis runs over, the one named last changes fastest.
Arguments:
- stress: float32 [8192, 512], P(('row', 'col')), may hold values from -2.5 to 2.5
- friction_state: float32 [8192, 512], P(('row', 'col')), may hold values from -0.5 to 0.5
- direct: float32 [8192, 512], P(('row', 'col')), may hold values from 0.5 to 1
- evolve: float32 [8192, 512], P(('row', 'col')), may hold values from 0.5 to 1
- relax_rate: float32 [8192, 512], P(('row', 'col')), may hold values from 0.2 to 1
- load_rate: float32 [8192, 512], P(('row', 'col')), may hold values from -4 to 4
- row_perm: int32 [64], P('row'), may hold values from 0 to 63, as said below
- patch_rows: int32 [64], P(('row', 'col')), may hold values from 0 to 15, as said below
- near_cols: int32 [64, 8, 7], P('row', 'col'), may hold values from -1 to 7, as said below
- near_blocks: bfloat16 [64, 8, 7, 128, 128], P('row', 'col'), may hold values from -0.0625 to 0.0625
- far_cols: int32 [64, 8, 9], P('row', 'col'), may hold values from 0 to 7
- far_ranks: int32 [64, 8, 9], P('row', 'col'), may hold values from 8 to 32
- far_left: bfloat16 [64, 8, 9, 32, 128], P('row', 'col'), may hold values from -0.125 to 0.125
- far_right: bfloat16 [64, 8, 9, 32, 128], P('row', 'col'), may hold values from -0.5 to 0.5
Outputs:
- stress_next: float32 [8192, 512], P(('row', 'col'))
- state_next: float32 [8192, 512], P(('row', 'col'))
The draws below stay inside these ranges and needn't reach their ends.
Inputs may be any that keep to these rules, and one draw needn't show every extreme that they name: `row_perm`: A permutation of the 64 blocks; each index of row holds, at positions r * 16 to (r + 1) * 16 - 1, exactly 2 blocks of every column group. `patch_rows`: for each index r of row, entries r * 16 to (r + 1) * 16 - 1 are a permutation of 0 to 15. `near_cols`: in each block row and column group the live slots come first, 1 to 7 of them, distinct; 7 live slots occur in every draw.
All inputs are finite; a program needn't handle non-finite values.
Results may differ from the reference program's by a relative error of at most 0.0038.
Values may be sent and summed in bfloat16 or wider, within the bound.
No kernel may reach another device: no remote copies, remote signals or barrier semaphores. Data moves between devices by JAX's collectives and lax.ppermute only.
A program may use at most 256 MiB of HBM per device.

```python
import math
import jax
import jax.numpy as jnp
from jax import lax

B = 128
R = 32
NPR = 7
FPR = 9
ENS = 512
PB = 2
NB = 64
NC = 8192
N_ROW = 4
N_COL = 8


def column_orders(key):
    block_total = PB * N_ROW * N_COL
    group_width = PB * N_ROW
    key_list = jax.random.split(key, block_total * N_COL)
    orders = jax.vmap(lambda one_key: jax.random.permutation(one_key, group_width))(key_list)
    return orders.reshape(block_total, N_COL, group_width).astype(jnp.int32)


def draw_row_perm(key, part):
    key = jax.random.fold_in(key, 11)
    group_width = PB * N_ROW
    key_list = jax.random.split(key, N_COL + N_ROW)
    inner = jax.vmap(lambda one_key: jax.random.permutation(one_key, group_width))(key_list[:N_COL])
    blocks = jnp.arange(N_COL, dtype=jnp.int32)[:, None] * group_width + inner.astype(jnp.int32)
    per_row = blocks.reshape(N_COL, N_ROW, PB).transpose(1, 0, 2).reshape(N_ROW, N_COL * PB)
    shuffle = jax.vmap(lambda one_key: jax.random.permutation(one_key, N_COL * PB))(key_list[N_COL:])
    return jnp.take_along_axis(per_row, shuffle.astype(jnp.int32), axis=1).reshape(-1).astype(jnp.int32)


def draw_patch_rows(key, part):
    key = jax.random.fold_in(key, 12)
    key_list = jax.random.split(key, N_ROW)
    shuffle = jax.vmap(lambda one_key: jax.random.permutation(one_key, N_COL * PB))(key_list)
    return shuffle.reshape(-1).astype(jnp.int32)


def draw_near_cols(key, part):
    orders = column_orders(key)
    key = jax.random.fold_in(key, 13)
    block_total = PB * N_ROW * N_COL
    rows_dev = PB * N_COL
    key_cap, key_count, key_row, key_col = jax.random.split(key, 4)
    device_caps = jax.random.randint(key_cap, (N_ROW, N_COL), 3, NPR + 1)
    raw_counts = jax.random.randint(key_count, (block_total, N_COL), 0, 1 << 20)
    counts = 1 + raw_counts % jnp.repeat(device_caps, rows_dev, axis=0)
    top_row = jax.random.randint(key_row, (), 0, block_total)
    top_col = jax.random.randint(key_col, (), 0, N_COL)
    counts = counts.at[top_row, top_col].set(NPR)
    slot_index = jnp.arange(NPR, dtype=jnp.int32)
    return jnp.where(slot_index[None, None, :] < counts[:, :, None], orders[:, :, :NPR], -1).astype(jnp.int32)


def draw_far_cols(key, part):
    orders = column_orders(key)
    group_width = PB * N_ROW
    picks = (NPR + jnp.arange(FPR, dtype=jnp.int32)) % group_width
    return orders[:, :, picks].astype(jnp.int32)


def with_ends(array, stream_key, least, largest):
    dims = array.shape
    place = [jax.random.randint(jax.random.fold_in(stream_key, axis), (), 0, dims[axis]) for axis in range(len(dims))]
    array = array.at[tuple(place)].set(least)
    longest = dims.index(max(dims))
    place[longest] = (place[longest] + 1) % dims[longest]
    return array.at[tuple(place)].set(largest)


def levels(stream_key, extent, cuts, smallest, top_value):
    def one(axis_at, blocks):
        heights = jax.random.uniform(jax.random.fold_in(jax.random.fold_in(stream_key, 6), axis_at), (blocks,), jnp.float32, smallest / len(cuts), top_value / len(cuts))
        return jnp.repeat(jnp.exp(heights), extent[axis_at] // blocks).reshape((-1,) + (1,) * (len(extent) - axis_at - 1))

    factor_of = one(*cuts[0])
    for cut in cuts[1:]:
        factor_of = factor_of * one(*cut)
    return factor_of


def noise(stream_key, shape, width, limit, cuts=(), held_as=jnp.bfloat16):
    values = width * jax.random.normal(stream_key, shape, jnp.float32)
    if cuts:
        values = values * levels(stream_key, shape, cuts, -0.22, 0.18)
    return jnp.clip(values, -limit, limit).astype(held_as)


def setup_inputs(seed: int = 0) -> dict:
    splits = jax.random.split(jax.random.key(seed), 15)
    return {
        "stress": noise(splits[0], (NC, ENS), 0.3, 2.5, ((0, 32),), jnp.float32),
        "friction_state": jnp.clip(jax.random.uniform(splits[1], (NC, ENS), jnp.float32, -0.5, 0.5) * levels(splits[1], (NC, ENS), ((0, 32),), -0.4, 0.0), -0.5, 0.5),
        "direct": jnp.clip(jnp.exp(math.log(1.0) - 0.6931472 * jax.random.uniform(splits[2], (NC, ENS), jnp.float32) ** levels(splits[2], (NC, ENS), ((0, 32),), -0.2, 0.2)), 0.5, 1.0),
        "evolve": jnp.clip(jnp.exp(math.log(1.0) - 0.6931472 * jax.random.uniform(splits[3], (NC, ENS), jnp.float32) ** levels(splits[3], (NC, ENS), ((0, 32),), -0.2, 0.2)), 0.5, 1.0),
        "relax_rate": jnp.clip(jnp.exp(math.log(1.0) - 1.609438 * jax.random.uniform(splits[4], (NC, ENS), jnp.float32) ** levels(splits[4], (NC, ENS), ((0, 32),), -0.2, 0.2)), 0.2, 1.0),
        "load_rate": noise(splits[5], (NC, ENS), 1.0, 4.0, ((0, 32),), jnp.float32),
        "row_perm": draw_row_perm(jax.random.fold_in(splits[14], 71), 0),
        "patch_rows": draw_patch_rows(jax.random.fold_in(splits[14], 71), 0),
        "near_cols": draw_near_cols(jax.random.fold_in(splits[14], 71), 0),
        "near_blocks": noise(splits[9], (NB, N_COL, NPR, B, B), (B * NPR * N_COL) ** -0.5, 0.0625, ((0, 4), (1, 8))),
        "far_cols": draw_far_cols(jax.random.fold_in(splits[14], 71), 0),
        "far_ranks": with_ends(jax.random.randint(splits[11], (NB, N_COL, FPR), R // 4, R + 1), jax.random.fold_in(splits[11], 1), R // 4, R).astype(jnp.int32),
        "far_left": noise(splits[12], (NB, N_COL, FPR, R, B), (R * FPR * N_COL) ** -0.5, 0.125, ((0, 4), (1, 8))),
        "far_right": noise(splits[13], (NB, N_COL, FPR, R, B), B ** -0.5, 0.5, ((0, 4), (1, 8))),
    }


TIME_STEP = 0.1
SECTION_SHIFT = 2.0 / 3.0
FIRST_WEIGHT = 0.25
SECOND_WEIGHT = 0.75


def slip_velocity(stress, friction_state, direct):
    return 2.0 * jnp.sinh(stress / direct) * jnp.exp(-friction_state / direct)


def patch_positions(patch_rows):
    total_blocks = patch_rows.shape[0]
    rows_dev = total_blocks // N_ROW
    return (jnp.arange(total_blocks, dtype=jnp.int32) // rows_dev) * rows_dev + patch_rows.astype(jnp.int32)


def kernel_apply(vel_b, row_perm, positions, near_cols, near_blocks, far_cols, far_ranks, far_left, far_right):
    total_blocks = row_perm.shape[0]
    blocks_of = row_perm[positions]
    natural = jnp.zeros((total_blocks, B, ENS), jnp.bfloat16).at[blocks_of].set(vel_b.reshape(total_blocks, B, ENS))
    group_width = total_blocks // N_COL
    offsets = jnp.arange(N_COL, dtype=jnp.int32)[:, None] * group_width
    rank_index = jnp.arange(R, dtype=jnp.int32)

    def one_row(pieces):
        near_index, near_data, far_index, rank_limit, left_data, right_data = pieces
        live_mask = (near_index >= 0).astype(jnp.float32)[:, :, None, None]
        near_x = natural[offsets + jnp.maximum(near_index, 0)].astype(jnp.float32) * live_mask
        near_part = jnp.einsum("ckab,ckbe->ae", near_data.astype(jnp.float32), near_x)
        far_x = natural[offsets + far_index].astype(jnp.float32)
        coeffs = jnp.einsum("ckrb,ckbe->ckre", right_data.astype(jnp.float32), far_x)
        coeffs = jnp.where(rank_index[None, None, :, None] < rank_limit[:, :, None, None], coeffs, 0.0)
        coeffs = lax.optimization_barrier(coeffs.astype(jnp.bfloat16)).astype(jnp.float32)
        return near_part + jnp.einsum("ckrb,ckre->be", left_data.astype(jnp.float32), coeffs)

    traction = lax.map(one_row, (near_cols, near_blocks, far_cols, far_ranks, far_left, far_right))
    return traction[positions].reshape(total_blocks * B, ENS)


def reference(stress, friction_state, direct, evolve, relax_rate, load_rate, row_perm, patch_rows, near_cols, near_blocks, far_cols, far_ranks, far_left, far_right):
    positions = patch_positions(patch_rows)

    def rates(stress_now, state_now):
        velocity = slip_velocity(stress_now, state_now, direct)
        traction = kernel_apply(velocity.astype(jnp.bfloat16), row_perm, positions, near_cols, near_blocks, far_cols, far_ranks, far_left, far_right)
        return load_rate - traction, relax_rate * (jnp.exp(-state_now / evolve) - velocity)

    first_stress, first_state = rates(stress, friction_state)
    stress_mid = stress + TIME_STEP * SECTION_SHIFT * first_stress
    state_mid = friction_state + TIME_STEP * SECTION_SHIFT * first_state
    second_stress, second_state = rates(stress_mid, state_mid)
    stress_next = stress + TIME_STEP * (FIRST_WEIGHT * first_stress + SECOND_WEIGHT * second_stress)
    state_next = friction_state + TIME_STEP * (FIRST_WEIGHT * first_state + SECOND_WEIGHT * second_state)
    return stress_next, state_next
```

```python
import functools

import jax
import jax.numpy as jnp
from jax import lax
from jax.experimental import pallas as pl
from jax.experimental.pallas import tpu as pltpu
from jax.sharding import PartitionSpec as P

TIME_STEP = 0.1
SECTION_SHIFT = 2.0 / 3.0
FIRST_WEIGHT = 0.25
SECOND_WEIGHT = 0.75
MID = TIME_STEP * SECTION_SHIFT
W1 = TIME_STEP * FIRST_WEIGHT
W2 = TIME_STEP * SECOND_WEIGHT
CHUNKS = 1

F32 = jnp.float32
BF16 = jnp.bfloat16
VMEM = pl.BlockSpec(memory_space=pltpu.VMEM)
SMEM = pl.BlockSpec(memory_space=pltpu.SMEM)
ANY = pl.BlockSpec(memory_space=pl.ANY)
LIMIT = 40 * 1024 * 1024


def params(limit=LIMIT):
    return pltpu.CompilerParams(vmem_limit_bytes=limit)


def cost(flops, nbytes, trans=0):
    return pl.CostEstimate(flops=int(flops), bytes_accessed=int(nbytes), transcendentals=int(trans))


def struct(shape, dtype):
    return jax.ShapeDtypeStruct(shape, dtype)


def plan_kernel(n_pair, n_row, patch_count, width, *refs):
    info = refs[0]
    patches = refs[1 : 1 + n_pair]
    perms = refs[1 + n_pair : 1 + n_pair + n_row]
    sel, arr, rows, inv = refs[1 + n_pair + n_row :]
    pair_patches = 2 * patch_count
    rows_dev = perms[0].shape[0]
    for m in range(n_pair):
        for i in range(pair_patches):
            q = patches[m][i]
            inv[q] = m * pair_patches + i
            rows[m * pair_patches + i] = q
    for side in range(2):
        group = info[1 + side]

        def pick(q, count):
            hit = lax.div(perms[0][q], width) == group

            @pl.when(hit)
            def _():
                sel[side * patch_count + count] = inv[q]

            return count + hit.astype(jnp.int32)

        lax.fori_loop(0, rows_dev, pick, jnp.int32(0))
    for s in range(n_row):

        def place(q, count):
            block = perms[s][q]
            hit = lax.div(block, width) == info[1]

            @pl.when(hit)
            def _():
                arr[lax.rem(block, width)] = s * patch_count + count

            return count + hit.astype(jnp.int32)

        lax.fori_loop(0, rows_dev, place, jnp.int32(0))


def make_plan(info, patches, perms, patch_count, width):
    n_pair, n_row = len(patches), len(perms)
    rows_dev = perms[0].shape[0]
    return pl.pallas_call(
        functools.partial(plan_kernel, n_pair, n_row, patch_count, width),
        out_shape=(
            struct((2 * patch_count,), jnp.int32),
            struct((width,), jnp.int32),
            struct((rows_dev,), jnp.int32),
        ),
        in_specs=[SMEM] * (1 + n_pair + n_row),
        out_specs=(SMEM,) * 3,
        scratch_shapes=[pltpu.SMEM((rows_dev,), jnp.int32)],
        cost_estimate=cost(1000, 1000),
        name="plan",
    )(info, *patches, *perms)


def build_kernel(rows, arr, near_cols, far_cols, far_ranks, near, left, right, out, spread, acc):
    slots, cell = near.shape[2], near.shape[3]
    far_slots, rank = left.shape[2], left.shape[3]
    q = rows[pl.program_id(0)]
    spread[...] = jnp.zeros_like(spread)
    ranks = lax.broadcasted_iota(jnp.int32, (rank, cell), 0)
    for k in range(far_slots):
        place = arr[far_cols[q * far_slots + k]]
        kept = jnp.where(ranks < far_ranks[q * far_slots + k], right[0, 0, k].astype(F32), 0.0)
        spread[pl.ds(k * rank, rank), pl.ds(pl.multiple_of(place * cell, cell), cell)] = kept.astype(BF16)
    acc[...] = lax.dot_general(
        left[0, 0].reshape(far_slots * rank, cell),
        spread[...],
        (((0,), (0,)), ((), ())),
        preferred_element_type=F32,
    )
    for k in range(slots):
        col = near_cols[q * slots + k]

        @pl.when(col >= 0)
        def _():
            at = pl.ds(pl.multiple_of(arr[jnp.maximum(col, 0)] * cell, cell), cell)
            acc[:, at] = acc[:, at] + near[0, 0, k].astype(F32)

    out[0] = acc[...].astype(BF16)


def build_matrix(rows, arr, near_cols, far_cols, far_ranks, near, left, right, n_pair):
    rows_dev, _, slots, cell, _ = near.shape
    far_slots, rank = left.shape[2], left.shape[3]
    depth = arr.shape[0] * cell
    per = rows_dev // n_pair

    def by_row(p, rows, *_):
        return (rows[p], 0, 0, 0, 0)

    return pl.pallas_call(
        build_kernel,
        out_shape=struct((n_pair, per * cell, depth), BF16),
        grid_spec=pltpu.PrefetchScalarGridSpec(
            num_scalar_prefetch=5,
            grid=(rows_dev,),
            in_specs=[
                pl.BlockSpec((1, 1, slots, cell, cell), by_row),
                pl.BlockSpec((1, 1, far_slots, rank, cell), by_row),
                pl.BlockSpec((1, 1, far_slots, rank, cell), by_row),
            ],
            out_specs=pl.BlockSpec((1, cell, depth), lambda p, *_: (p // per, p % per, 0)),
            scratch_shapes=[
                pltpu.VMEM((far_slots * rank, depth), BF16),
                pltpu.VMEM((cell, depth), F32),
            ],
        ),
        compiler_params=params(),
        cost_estimate=cost(
            2 * rows_dev * cell * far_slots * rank * depth, 2 * (near.size + left.size + right.size) + 2 * rows_dev * cell * depth
        ),
        name="build_matrix",
    )(rows, arr, near_cols, far_cols, far_ranks, near, left, right)


def pick_kernel(pair_patches, cell, sel, *refs):
    n_pair = len(refs) - 2
    sources, out, sems = refs[:n_pair], refs[n_pair], refs[n_pair + 1]
    for t in range(pair_patches):
        which = lax.div(sel[t], pair_patches)
        block = pl.multiple_of(lax.rem(sel[t], pair_patches) * cell, cell)
        for m in range(n_pair):

            @pl.when(which == m)
            def _():
                pltpu.make_async_copy(
                    sources[m].at[pl.ds(block, cell)], out.at[pl.ds(t * cell, cell)], sems.at[t]
                ).start()

    for t in range(pair_patches):
        pltpu.make_async_copy(
            sources[0].at[pl.ds(0, cell)], out.at[pl.ds(t * cell, cell)], sems.at[t]
        ).wait()


def pick(sel, sources, cell):
    pair_patches = sel.shape[0]
    return pl.pallas_call(
        functools.partial(pick_kernel, pair_patches, cell),
        out_shape=struct(sources[0].shape, BF16),
        in_specs=[SMEM] + [ANY] * len(sources),
        out_specs=ANY,
        scratch_shapes=[pltpu.SemaphoreType.DMA((pair_patches,))],
        cost_estimate=cost(0, 4 * sources[0].size),
        name="pick",
    )(sel, *sources)


def apply_kernel(n_pair, n_row, m_own, m_sib, *refs):
    pieces = refs[:n_row]
    outs = refs[n_row : n_row + n_pair]
    x_own, x_sib = refs[n_row + n_pair :]
    half = pieces[0].shape[0] // 2
    step = pl.program_id(0)

    @pl.when(step == 0)
    def _():
        for s in range(n_row):
            x_own[pl.ds(s * half, half)] = pieces[s][pl.ds(0, half)]
            x_sib[pl.ds(s * half, half)] = pieces[s][pl.ds(half, half)]

    total = jnp.dot(m_own[0], x_own[...], preferred_element_type=F32)
    total = total + jnp.dot(m_sib[0], x_sib[...], preferred_element_type=F32)
    for m in range(n_pair):

        @pl.when(step == m)
        def _():
            outs[m][...] = total.astype(outs[m].dtype)


def apply_matrix(m_own, m_sib, pieces):
    n_pair, high, depth = m_own.shape
    lanes = pieces[0].shape[1]
    block = pl.BlockSpec((1, high, depth), lambda m: (m, 0, 0))
    whole = pl.BlockSpec(pieces[0].shape, lambda m: (0, 0))
    return pl.pallas_call(
        functools.partial(apply_kernel, n_pair, len(pieces)),
        out_shape=tuple(struct((high, lanes), F32 if m == 0 else BF16) for m in range(n_pair)),
        grid=(n_pair,),
        in_specs=[block, block] + [whole] * len(pieces),
        out_specs=tuple(pl.BlockSpec((high, lanes), lambda m: (0, 0)) for _ in range(n_pair)),
        scratch_shapes=[pltpu.VMEM((depth, lanes), BF16)] * 2,
        compiler_params=params(),
        cost_estimate=cost(4 * n_pair * high * depth * lanes, 4 * m_own.size),
        name="apply_matrix",
    )(m_own, m_sib, *pieces)


def start_kernel(chunks, info, stress, state, direct, *outs):
    keep, give = outs[:chunks], outs[chunks:]
    half = stress.shape[1] // 2
    lanes = half // chunks
    side = info[0]
    for own, refs in ((False, give), (True, keep)):
        base = (side if own else 1 - side) * half
        for j in range(chunks):
            at = pl.ds(pl.multiple_of(base + j * lanes, lanes), lanes)
            inverse = 1.0 / direct[:, at]
            stress_now, state_now = stress[:, at], state[:, at]
            velocity = jnp.exp((stress_now - state_now) * inverse) - jnp.exp((-stress_now - state_now) * inverse)
            refs[j][...] = velocity.astype(BF16)


def start(info, stress, state, direct, chunks):
    high, members = stress.shape
    lanes = members // 2 // chunks
    tile = 128
    return pl.pallas_call(
        functools.partial(start_kernel, chunks),
        out_shape=(struct((high, lanes), BF16),) * (2 * chunks),
        grid=(high // tile,),
        in_specs=[SMEM] + [pl.BlockSpec((tile, members), lambda i: (i, 0))] * 3,
        out_specs=(pl.BlockSpec((tile, lanes), lambda i: (i, 0)),) * (2 * chunks),
        cost_estimate=cost(10 * stress.size, 14 * stress.size, 3 * stress.size),
        name="start",
    )(info, stress, state, direct)


def mid_kernel(chunks, info, stress, state, direct, evolve, relax, load, keep, give, base, state_base):
    half = stress.shape[1] // 2
    lanes = half // chunks
    side = info[0]
    for own, ref in ((True, keep), (False, give)):
        first = (side if own else 1 - side) * half
        for j in range(chunks):
            at = pl.ds(pl.multiple_of(first + j * lanes, lanes), lanes)
            inverse = 1.0 / direct[:, at]
            inverse_e = 1.0 / evolve[:, at]
            stress_now, state_now = stress[:, at], state[:, at]
            relax_now, load_now = relax[:, at], load[:, at]
            velocity = jnp.exp((stress_now - state_now) * inverse) - jnp.exp((-stress_now - state_now) * inverse)
            state_rate = relax_now * (jnp.exp(-state_now * inverse_e) - velocity)
            state_mid = state_now + MID * state_rate
            ref[j, 0] = stress_now + MID * load_now
            ref[j, 1] = inverse
            ref[j, 2] = jnp.exp(-state_mid * inverse)
            base[:, at] = stress_now + TIME_STEP * load_now
            state_base[:, at] = state_now + W1 * state_rate + W2 * relax_now * jnp.exp(-state_mid * inverse_e)


def mid(info, stress, state, direct, evolve, relax, load, chunks):
    high, members = stress.shape
    lanes = members // 2 // chunks
    tile = 128
    wide = pl.BlockSpec((tile, members), lambda i: (i, 0))
    split = pl.BlockSpec((chunks, 3, tile, lanes), lambda i: (0, 0, i, 0))
    return pl.pallas_call(
        functools.partial(mid_kernel, chunks),
        out_shape=(struct((chunks, 3, high, lanes), F32),) * 2 + (struct(stress.shape, F32),) * 2,
        grid=(high // tile,),
        in_specs=[SMEM] + [wide] * 6,
        out_specs=(split, split, wide, wide),
        cost_estimate=cost(20 * stress.size, 44 * stress.size, 6 * stress.size),
        name="mid",
    )(info, stress, state, direct, evolve, relax, load)


def merge_kernel(info, keep, recv, out):
    high = keep.shape[0]
    side = info[0]
    out[pl.ds(pl.multiple_of(side * high, high), high)] = keep[...]
    out[pl.ds(pl.multiple_of((1 - side) * high, high), high)] = recv[...]


def merge(info, keep, recv):
    high, lanes = keep.shape
    return pl.pallas_call(
        merge_kernel,
        out_shape=struct((2 * high, lanes), keep.dtype),
        in_specs=[SMEM, VMEM, VMEM],
        out_specs=VMEM,
        cost_estimate=cost(0, 8 * keep.size),
        name="merge",
    )(info, keep, recv)


def second_kernel(info, keep, recv, *refs):
    n_pair = len(refs) - 4
    parts = refs[:n_pair]
    total_out, vel_b, vel_keep, vel_give = refs[n_pair:]
    high = keep.shape[2]
    side = info[0]
    for own, held, vel_out in ((True, keep, vel_keep), (False, recv, vel_give)):
        at = pl.ds(pl.multiple_of((side if own else 1 - side) * high, high), high)
        total = parts[0][at]
        for m in range(1, n_pair):
            total = total + parts[m][at].astype(F32)
        total_out[at] = W1 * total
        scaled = (held[0, 0] - MID * total) * held[0, 1]
        velocity = held[0, 2] * (jnp.exp(scaled) - jnp.exp(-scaled))
        vel_b[at] = velocity.astype(BF16)
        vel_out[...] = velocity


def second(info, keep, recv, parts, chunk):
    high, lanes = parts[0].shape
    held = pl.BlockSpec((1, 3, high // 2, lanes), lambda i: (chunk, 0, 0, 0))
    whole = pl.BlockSpec((high, lanes), lambda i: (0, 0))
    half = pl.BlockSpec((high // 2, lanes), lambda i: (0, 0))
    return pl.pallas_call(
        second_kernel,
        out_shape=(struct((high, lanes), F32), struct((high, lanes), BF16))
        + (struct((high // 2, lanes), F32),) * 2,
        grid=(1,),
        in_specs=[SMEM, held, held] + [whole] * len(parts),
        out_specs=(whole, whole, half, half),
        cost_estimate=cost(10 * high * lanes, 40 * high * lanes, 2 * high * lanes),
        name="second",
    )(info, keep, recv, *parts)


def weigh_kernel(info, first, *refs):
    parts = refs[:-2]
    keep, give = refs[-2:]
    high = keep.shape[0]
    side = info[0]
    for own, ref in ((False, give), (True, keep)):
        at = pl.ds(pl.multiple_of((side if own else 1 - side) * high, high), high)
        total = parts[0][at]
        for part in parts[1:]:
            total = total + part[at].astype(F32)
        ref[...] = first[at] + W2 * total


def weigh(info, first, parts):
    high, lanes = first.shape
    return pl.pallas_call(
        weigh_kernel,
        out_shape=(struct((high // 2, lanes), F32),) * 2,
        in_specs=[SMEM] + [VMEM] * (1 + len(parts)),
        out_specs=(VMEM, VMEM),
        cost_estimate=cost(10 * high * lanes, 20 * high * lanes),
        name="weigh",
    )(info, first, *parts)


def finish_kernel(chunks, scaled, info, base, *refs):
    out = refs[-1]
    factor = refs[0] if scaled else None
    pieces = refs[1:-1] if scaled else refs[:-1]
    half = base.shape[1] // 2
    lanes = half // chunks
    side = info[0]
    for j in range(chunks):
        for own, piece in ((True, pieces[j]), (False, pieces[chunks + j])):
            first = (side if own else 1 - side) * half + j * lanes
            at = pl.ds(pl.multiple_of(first, lanes), lanes)
            change = piece[...]
            if scaled:
                change = W2 * factor[:, at] * change
            out[:, at] = base[:, at] - change


def finish(info, base, factor, keeps, recvs):
    chunks = len(keeps)
    scaled = factor is not None
    extra = [factor] if scaled else []
    return pl.pallas_call(
        functools.partial(finish_kernel, chunks, scaled),
        out_shape=struct(base.shape, F32),
        in_specs=[SMEM] + [VMEM] * (1 + len(extra) + 2 * chunks),
        out_specs=VMEM,
        cost_estimate=cost(3 * base.size, 16 * base.size),
        name="finish",
    )(info, base, *extra, *keeps, *recvs)


def shards(
    stress,
    friction_state,
    direct,
    evolve,
    relax_rate,
    load_rate,
    row_perm,
    patch_rows,
    near_cols,
    near_blocks,
    far_cols,
    far_ranks,
    far_left,
    far_right,
):
    n_col, n_row = lax.axis_size("col"), lax.axis_size("row")
    n_pair = n_col // 2
    rows_dev = row_perm.shape[0]
    patch_count = patch_rows.shape[0]
    width = rows_dev * n_row // n_col
    cell = near_blocks.shape[-1]
    col = lax.axis_index("col")
    side = col % 2
    info = jnp.stack([side, col, col + 1 - 2 * side]).astype(jnp.int32)

    def swap(x):
        return lax.ppermute(x, "col", [(i, i ^ 1) for i in range(n_col)])

    def across(x, m):
        return lax.ppermute(x, "col", [(i, i ^ (2 * m)) for i in range(n_col)])

    def along(x, s):
        return lax.ppermute(x, "row", [(i, (i + s) % n_row) for i in range(n_row)])

    both = jnp.stack([patch_rows, swap(patch_rows)])
    both = jnp.where(side == 0, both, both[::-1]).reshape(-1)
    patches = [both] + [across(both, m) for m in range(1, n_pair)]
    perms = [row_perm] + [along(row_perm, s) for s in range(1, n_row)]
    sel, arr, rows = make_plan(info, patches, perms, patch_count, width)

    started = start(info, stress, friction_state, direct, CHUNKS)
    keep_first, give_first = started[:CHUNKS], started[CHUNKS:]
    keep_mid, give_mid, base, state_base = mid(
        info, stress, friction_state, direct, evolve, relax_rate, load_rate, CHUNKS
    )
    recv_mid = swap(give_mid)
    m_own = build_matrix(
        rows,
        arr,
        near_cols.reshape(-1),
        far_cols.reshape(-1),
        far_ranks.reshape(-1),
        near_blocks,
        far_left,
        far_right,
        n_pair,
    )
    m_sib = swap(m_own)

    def traction_parts(vel_b):
        sources = [vel_b] + [across(vel_b, m) for m in range(1, n_pair)]
        chosen = pick(sel, sources, cell)
        pieces = [chosen] + [along(chosen, s) for s in range(1, n_row)]
        partial = apply_matrix(m_own, m_sib, pieces)
        return [partial[0]] + [across(partial[m], m) for m in range(1, n_pair)]

    keeps, recvs, vel_keeps, vel_recvs = [], [], [], []
    for j in range(CHUNKS):
        vel_b = merge(info, keep_first[j], swap(give_first[j]))
        parts = traction_parts(vel_b)
        first, vel_b, vel_keep, vel_give = second(info, keep_mid, recv_mid, parts, j)
        vel_keeps.append(vel_keep)
        vel_recvs.append(swap(vel_give))
        parts = traction_parts(vel_b)
        keep, give = weigh(info, first, parts)
        keeps.append(keep)
        recvs.append(swap(give))
    state_next = finish(info, state_base, relax_rate, vel_keeps, vel_recvs)
    stress_next = finish(info, base, None, keeps, recvs)
    return (stress_next, state_next)


def solution(mesh):
    cells = P(("row", "col"), None)
    placed = (
        cells,
        cells,
        cells,
        cells,
        cells,
        cells,
        P("row"),
        P(("row", "col")),
        P("row", "col", None),
        P("row", "col", None, None, None),
        P("row", "col", None),
        P("row", "col", None),
        P("row", "col", None, None, None),
        P("row", "col", None, None, None),
    )
    return jax.shard_map(
        shards,
        mesh=mesh,
        in_specs=placed,
        out_specs=(cells, cells),
        check_vma=False,
    )
```

```python
import functools

import jax
import jax.numpy as jnp
from jax import lax
from jax.experimental import pallas as pl
from jax.experimental.pallas import tpu as pltpu
from jax.sharding import PartitionSpec as P

TIME_STEP = 0.1
SECTION_SHIFT = 2.0 / 3.0
FIRST_WEIGHT = 0.25
SECOND_WEIGHT = 0.75
MID = TIME_STEP * SECTION_SHIFT
W1 = TIME_STEP * FIRST_WEIGHT
W2 = TIME_STEP * SECOND_WEIGHT
CHUNKS = 1

F32 = jnp.float32
BF16 = jnp.bfloat16
VMEM = pl.BlockSpec(memory_space=pltpu.VMEM)
SMEM = pl.BlockSpec(memory_space=pltpu.SMEM)
ANY = pl.BlockSpec(memory_space=pl.ANY)
LIMIT = 16 * 1024 * 1024


def params(limit=LIMIT):
    return pltpu.CompilerParams(vmem_limit_bytes=limit)


def cost(flops, nbytes, trans=0):
    return pl.CostEstimate(flops=int(flops), bytes_accessed=int(nbytes), transcendentals=int(trans))


def struct(shape, dtype):
    return jax.ShapeDtypeStruct(shape, dtype)


def plan_kernel(n_pair, n_row, patch_count, width, *refs):
    patches = refs[:n_pair]
    perms = refs[n_pair : n_pair + n_row]
    sel, arr, rows, inv = refs[n_pair + n_row :]
    pair_patches = 2 * patch_count
    rows_dev = perms[0].shape[0]
    col = lax.axis_index("col")
    side = lax.rem(col, 2)
    groups = (col, col + 1 - 2 * side)
    for m in range(n_pair):
        for i in range(pair_patches):
            q = patches[m][lax.rem(i + side * patch_count, pair_patches)]
            inv[q] = m * pair_patches + i
            rows[m * pair_patches + i] = q
    for n, group in enumerate(groups):

        def pick(q, count, n=n, group=group):
            hit = lax.div(perms[0][q], width) == group

            @pl.when(hit)
            def _():
                sel[n * patch_count + count] = inv[q]

            return count + hit.astype(jnp.int32)

        lax.fori_loop(0, rows_dev, pick, jnp.int32(0))
    for s in range(n_row):

        def place(q, count):
            block = perms[s][q]
            hit = lax.div(block, width) == groups[0]

            @pl.when(hit)
            def _():
                arr[lax.rem(block, width)] = s * patch_count + count

            return count + hit.astype(jnp.int32)

        lax.fori_loop(0, rows_dev, place, jnp.int32(0))


def make_plan(patches, perms, patch_count, width):
    n_pair, n_row = len(patches), len(perms)
    rows_dev = perms[0].shape[0]
    return pl.pallas_call(
        functools.partial(plan_kernel, n_pair, n_row, patch_count, width),
        out_shape=(
            struct((2 * patch_count,), jnp.int32),
            struct((width,), jnp.int32),
            struct((rows_dev,), jnp.int32),
        ),
        in_specs=[SMEM] * (n_pair + n_row),
        out_specs=(SMEM,) * 3,
        scratch_shapes=[pltpu.SMEM((rows_dev,), jnp.int32)],
        compiler_params=params(),
        cost_estimate=cost(1000, 1000),
        name="plan",
    )(*patches, *perms)


def build_kernel(rows, arr, near_cols, far_cols, far_ranks, near, left, right, out, spread, acc):
    slots, cell = near.shape[2], near.shape[3]
    far_slots, rank = left.shape[2], left.shape[3]
    q = rows[pl.program_id(0)]
    spread[...] = jnp.zeros_like(spread)
    ranks = lax.broadcasted_iota(jnp.int32, (rank, cell), 0)
    for k in range(far_slots):
        place = arr[far_cols[q * far_slots + k]]
        kept = jnp.where(ranks < far_ranks[q * far_slots + k], right[0, 0, k].astype(F32), 0.0)
        spread[pl.ds(k * rank, rank), pl.ds(pl.multiple_of(place * cell, cell), cell)] = kept.astype(BF16)
    acc[...] = lax.dot_general(
        left[0, 0].reshape(far_slots * rank, cell),
        spread[...],
        (((0,), (0,)), ((), ())),
        preferred_element_type=F32,
    )
    for k in range(slots):
        col = near_cols[q * slots + k]

        @pl.when(col >= 0)
        def _():
            at = pl.ds(pl.multiple_of(arr[jnp.maximum(col, 0)] * cell, cell), cell)
            acc[:, at] = acc[:, at] + near[0, 0, k].astype(F32)

    out[0] = acc[...].astype(BF16)


def build_matrix(rows, arr, near_cols, far_cols, far_ranks, near, left, right, n_pair):
    rows_dev, _, slots, cell, _ = near.shape
    far_slots, rank = left.shape[2], left.shape[3]
    depth = arr.shape[0] * cell
    per = rows_dev // n_pair

    def by_row(p, rows, *_):
        return (rows[p], 0, 0, 0, 0)

    return pl.pallas_call(
        build_kernel,
        out_shape=struct((n_pair, per * cell, depth), BF16),
        grid_spec=pltpu.PrefetchScalarGridSpec(
            num_scalar_prefetch=5,
            grid=(rows_dev,),
            in_specs=[
                pl.BlockSpec((1, 1, slots, cell, cell), by_row),
                pl.BlockSpec((1, 1, far_slots, rank, cell), by_row),
                pl.BlockSpec((1, 1, far_slots, rank, cell), by_row),
            ],
            out_specs=pl.BlockSpec((1, cell, depth), lambda p, *_: (p // per, p % per, 0)),
            scratch_shapes=[
                pltpu.VMEM((far_slots * rank, depth), BF16),
                pltpu.VMEM((cell, depth), F32),
            ],
        ),
        compiler_params=params(56 * 1024 * 1024),
        cost_estimate=cost(
            2 * rows_dev * cell * far_slots * rank * depth, 2 * (near.size + left.size + right.size) + 2 * rows_dev * cell * depth
        ),
        name="build_matrix",
    )(rows, arr, near_cols, far_cols, far_ranks, near, left, right)


def pick_kernel(pair_patches, cell, sel, *refs):
    sources, out = refs[:-1], refs[-1]
    for t in range(pair_patches):
        which = lax.div(sel[t], pair_patches)
        block = pl.multiple_of(lax.rem(sel[t], pair_patches) * cell, cell)
        for m, source in enumerate(sources):

            @pl.when(which == m)
            def _():
                out[pl.ds(t * cell, cell)] = source[pl.ds(block, cell)]


def pick(sel, sources, cell):
    pair_patches = sel.shape[0]
    return pl.pallas_call(
        functools.partial(pick_kernel, pair_patches, cell),
        out_shape=struct(sources[0].shape, BF16),
        in_specs=[SMEM] + [VMEM] * len(sources),
        out_specs=VMEM,
        compiler_params=params(),
        cost_estimate=cost(0, 4 * sources[0].size),
        name="pick",
    )(sel, *sources)


def apply_kernel(n_pair, n_row, m_own, m_sib, *refs):
    pieces = refs[:n_row]
    outs = refs[n_row : n_row + n_pair]
    x_own, x_sib = refs[n_row + n_pair :]
    half = pieces[0].shape[0] // 2
    step = pl.program_id(0)

    @pl.when(step == 0)
    def _():
        for s in range(n_row):
            x_own[pl.ds(s * half, half)] = pieces[s][pl.ds(0, half)]
            x_sib[pl.ds(s * half, half)] = pieces[s][pl.ds(half, half)]

    total = jnp.dot(m_own[0], x_own[...], preferred_element_type=F32)
    total = total + jnp.dot(m_sib[0], x_sib[...], preferred_element_type=F32)
    for m in range(n_pair):

        @pl.when(step == m)
        def _():
            outs[m][...] = total.astype(outs[m].dtype)


def apply_matrix(m_own, m_sib, pieces):
    n_pair, high, depth = m_own.shape
    lanes = pieces[0].shape[1]
    block = pl.BlockSpec((1, high, depth), lambda m: (m, 0, 0))
    whole = pl.BlockSpec(pieces[0].shape, lambda m: (0, 0))
    return pl.pallas_call(
        functools.partial(apply_kernel, n_pair, len(pieces)),
        out_shape=tuple(struct((high, lanes), F32 if m == 0 else BF16) for m in range(n_pair)),
        grid=(n_pair,),
        in_specs=[block, block] + [whole] * len(pieces),
        out_specs=tuple(pl.BlockSpec((high, lanes), lambda m: (0, 0)) for _ in range(n_pair)),
        scratch_shapes=[pltpu.VMEM((depth, lanes), BF16)] * 2,
        compiler_params=params(),
        cost_estimate=cost(4 * n_pair * high * depth * lanes, 4 * m_own.size),
        name="apply_matrix",
    )(m_own, m_sib, *pieces)


def start_kernel(chunks, stress, state, direct, *outs):
    keep, give = outs[:chunks], outs[chunks:]
    half = stress.shape[1] // 2
    lanes = half // chunks
    side = lax.rem(lax.axis_index("col"), 2)
    for own, refs in ((False, give), (True, keep)):
        base = (side if own else 1 - side) * half
        for j in range(chunks):
            at = pl.ds(pl.multiple_of(base + j * lanes, lanes), lanes)
            inverse = 1.0 / direct[:, at]
            stress_now, state_now = stress[:, at], state[:, at]
            velocity = jnp.exp((stress_now - state_now) * inverse) - jnp.exp((-stress_now - state_now) * inverse)
            refs[j][...] = velocity.astype(BF16)


def start(stress, state, direct, chunks):
    high, members = stress.shape
    lanes = members // 2 // chunks
    tile = 128
    return pl.pallas_call(
        functools.partial(start_kernel, chunks),
        out_shape=(struct((high, lanes), BF16),) * (2 * chunks),
        grid=(high // tile,),
        in_specs=[pl.BlockSpec((tile, members), lambda i: (i, 0))] * 3,
        out_specs=(pl.BlockSpec((tile, lanes), lambda i: (i, 0)),) * (2 * chunks),
        compiler_params=params(),
        cost_estimate=cost(10 * stress.size, 14 * stress.size, 3 * stress.size),
        name="start",
    )(stress, state, direct)


def mid_kernel(chunks, stress, state, direct, evolve, relax, load, keep, give, base, state_base):
    half = stress.shape[1] // 2
    lanes = half // chunks
    side = lax.rem(lax.axis_index("col"), 2)
    for own, ref in ((True, keep), (False, give)):
        first = (side if own else 1 - side) * half
        for j in range(chunks):
            at = pl.ds(pl.multiple_of(first + j * lanes, lanes), lanes)
            inverse = 1.0 / direct[:, at]
            inverse_e = 1.0 / evolve[:, at]
            stress_now, state_now = stress[:, at], state[:, at]
            relax_now, load_now = relax[:, at], load[:, at]
            velocity = jnp.exp((stress_now - state_now) * inverse) - jnp.exp((-stress_now - state_now) * inverse)
            state_rate = relax_now * (jnp.exp(-state_now * inverse_e) - velocity)
            state_mid = state_now + MID * state_rate
            ref[j, 0] = stress_now + MID * load_now
            ref[j, 1] = inverse
            ref[j, 2] = jnp.exp(-state_mid * inverse)
            base[:, at] = stress_now + TIME_STEP * load_now
            state_base[:, at] = state_now + W1 * state_rate + W2 * relax_now * jnp.exp(-state_mid * inverse_e)


def mid(stress, state, direct, evolve, relax, load, chunks):
    high, members = stress.shape
    lanes = members // 2 // chunks
    tile = 128
    wide = pl.BlockSpec((tile, members), lambda i: (i, 0))
    split = pl.BlockSpec((chunks, 3, tile, lanes), lambda i: (0, 0, i, 0))
    return pl.pallas_call(
        functools.partial(mid_kernel, chunks),
        out_shape=(struct((chunks, 3, high, lanes), F32),) * 2 + (struct(stress.shape, F32),) * 2,
        grid=(high // tile,),
        in_specs=[wide] * 6,
        out_specs=(split, split, wide, wide),
        compiler_params=params(),
        cost_estimate=cost(20 * stress.size, 44 * stress.size, 6 * stress.size),
        name="mid",
    )(stress, state, direct, evolve, relax, load)


def merge_kernel(keep, recv, out):
    high = keep.shape[0]
    side = lax.rem(lax.axis_index("col"), 2)
    out[pl.ds(pl.multiple_of(side * high, high), high)] = keep[...]
    out[pl.ds(pl.multiple_of((1 - side) * high, high), high)] = recv[...]


def merge(keep, recv):
    high, lanes = keep.shape
    return pl.pallas_call(
        merge_kernel,
        out_shape=struct((2 * high, lanes), keep.dtype),
        in_specs=[VMEM, VMEM],
        out_specs=VMEM,
        compiler_params=params(),
        cost_estimate=cost(0, 8 * keep.size),
        name="merge",
    )(keep, recv)


def second_kernel(keep, recv, *refs):
    n_pair = len(refs) - 4
    parts = refs[:n_pair]
    total_out, vel_b, vel_keep, vel_give = refs[n_pair:]
    high = keep.shape[2]
    side = lax.rem(lax.axis_index("col"), 2)
    for own, held, vel_out in ((True, keep, vel_keep), (False, recv, vel_give)):
        at = pl.ds(pl.multiple_of((side if own else 1 - side) * high, high), high)
        total = parts[0][at]
        for m in range(1, n_pair):
            total = total + parts[m][at].astype(F32)
        total_out[at] = W1 * total
        scaled = (held[0, 0] - MID * total) * held[0, 1]
        velocity = held[0, 2] * (jnp.exp(scaled) - jnp.exp(-scaled))
        vel_b[at] = velocity.astype(BF16)
        vel_out[...] = velocity


def second(keep, recv, parts, chunk):
    high, lanes = parts[0].shape
    held = pl.BlockSpec((1, 3, high // 2, lanes), lambda i: (chunk, 0, 0, 0))
    whole = pl.BlockSpec((high, lanes), lambda i: (0, 0))
    half = pl.BlockSpec((high // 2, lanes), lambda i: (0, 0))
    return pl.pallas_call(
        second_kernel,
        out_shape=(struct((high, lanes), F32), struct((high, lanes), BF16))
        + (struct((high // 2, lanes), F32),) * 2,
        grid=(1,),
        in_specs=[held, held] + [whole] * len(parts),
        out_specs=(whole, whole, half, half),
        compiler_params=params(),
        cost_estimate=cost(10 * high * lanes, 40 * high * lanes, 2 * high * lanes),
        name="second",
    )(keep, recv, *parts)


def weigh_kernel(first, *refs):
    parts = refs[:-2]
    keep, give = refs[-2:]
    high = keep.shape[0]
    side = lax.rem(lax.axis_index("col"), 2)
    for own, ref in ((False, give), (True, keep)):
        at = pl.ds(pl.multiple_of((side if own else 1 - side) * high, high), high)
        total = parts[0][at]
        for part in parts[1:]:
            total = total + part[at].astype(F32)
        ref[...] = first[at] + W2 * total


def weigh(first, parts):
    high, lanes = first.shape
    return pl.pallas_call(
        weigh_kernel,
        out_shape=(struct((high // 2, lanes), F32),) * 2,
        in_specs=[VMEM] * (1 + len(parts)),
        out_specs=(VMEM, VMEM),
        compiler_params=params(),
        cost_estimate=cost(10 * high * lanes, 20 * high * lanes),
        name="weigh",
    )(first, *parts)


def finish_kernel(chunks, scaled, base, *refs):
    out = refs[-1]
    factor = refs[0] if scaled else None
    pieces = refs[1:-1] if scaled else refs[:-1]
    half = base.shape[1] // 2
    lanes = half // chunks
    side = lax.rem(lax.axis_index("col"), 2)
    for j in range(chunks):
        for own, piece in ((True, pieces[j]), (False, pieces[chunks + j])):
            first = (side if own else 1 - side) * half + j * lanes
            at = pl.ds(pl.multiple_of(first, lanes), lanes)
            change = piece[...]
            if scaled:
                change = W2 * factor[:, at] * change
            out[:, at] = base[:, at] - change


def finish(base, factor, keeps, recvs):
    chunks = len(keeps)
    scaled = factor is not None
    extra = [factor] if scaled else []
    return pl.pallas_call(
        functools.partial(finish_kernel, chunks, scaled),
        out_shape=struct(base.shape, F32),
        in_specs=[VMEM] * (1 + len(extra) + 2 * chunks),
        out_specs=VMEM,
        compiler_params=params(),
        cost_estimate=cost(3 * base.size, 16 * base.size),
        name="finish",
    )(base, *extra, *keeps, *recvs)


def shards(
    stress,
    friction_state,
    direct,
    evolve,
    relax_rate,
    load_rate,
    row_perm,
    patch_rows,
    near_cols,
    near_blocks,
    far_cols,
    far_ranks,
    far_left,
    far_right,
):
    n_col, n_row = lax.axis_size("col"), lax.axis_size("row")
    n_pair = n_col // 2
    rows_dev = row_perm.shape[0]
    patch_count = patch_rows.shape[0]
    width = rows_dev * n_row // n_col
    cell = near_blocks.shape[-1]

    def after(values, dep):
        return lax.optimization_barrier((values, dep))[0]

    def swap(x):
        return lax.ppermute(x, "col", [(i, i ^ 1) for i in range(n_col)])

    def across(x, m):
        return lax.ppermute(x, "col", [(i, i ^ (2 * m)) for i in range(n_col)])

    def along(x, s):
        return lax.ppermute(x, "row", [(i, (i + s) % n_row) for i in range(n_row)])

    started = start(stress, friction_state, direct, CHUNKS)
    keep_first, give_first = started[:CHUNKS], started[CHUNKS:]
    recv_first = [swap(give) for give in give_first]
    rows_mine, perm_mine = after((patch_rows, row_perm), give_first[0])
    both = jnp.concatenate([rows_mine, swap(rows_mine)])
    patches = [both] + [across(both, m) for m in range(1, n_pair)]
    perms = [perm_mine] + [along(perm_mine, s) for s in range(1, n_row)]
    sel, arr, rows = make_plan(patches, perms, patch_count, width)

    vel_first = [merge(keep, recv) for keep, recv in zip(keep_first, recv_first)]
    tables = after((near_cols, far_cols, far_ranks), vel_first[0])
    m_own = build_matrix(rows, arr, *[t.reshape(-1) for t in tables], near_blocks, far_left, far_right, n_pair)
    m_sib = swap(m_own)

    def route(vel_b):
        sources = [vel_b] + [across(vel_b, m) for m in range(1, n_pair)]
        return pick(sel, sources, cell)

    def traction_parts(chosen):
        pieces = [chosen] + [along(chosen, s) for s in range(1, n_row)]
        partial = apply_matrix(m_own, m_sib, pieces)
        return [partial[0]] + [across(partial[m], m) for m in range(1, n_pair)]

    chosen_first = [route(vel_b) for vel_b in vel_first]
    held = (stress, friction_state, direct, evolve, relax_rate, load_rate)
    keep_mid, give_mid, base, state_base = mid(*after(held, chosen_first[0]), CHUNKS)
    recv_mid = swap(give_mid)
    keeps, recvs, vel_keeps, vel_recvs = [], [], [], []
    for j in range(CHUNKS):
        parts = traction_parts(chosen_first[j])
        first, vel_b, vel_keep, vel_give = second(keep_mid, recv_mid, parts, j)
        vel_keeps.append(vel_keep)
        vel_recvs.append(swap(vel_give))
        parts = traction_parts(route(vel_b))
        keep, give = weigh(first, parts)
        keeps.append(keep)
        recvs.append(swap(give))
    state_next = finish(state_base, relax_rate, vel_keeps, vel_recvs)
    stress_next = finish(base, None, keeps, recvs)
    return (stress_next, state_next)


def solution(mesh):
    cells = P(("row", "col"), None)
    placed = (
        cells,
        cells,
        cells,
        cells,
        cells,
        cells,
        P("row"),
        P(("row", "col")),
        P("row", "col", None),
        P("row", "col", None, None, None),
        P("row", "col", None),
        P("row", "col", None),
        P("row", "col", None, None, None),
        P("row", "col", None, None, None),
    )
    return jax.shard_map(
        shards,
        mesh=mesh,
        in_specs=placed,
        out_specs=(cells, cells),
        check_vma=False,
    )
```

```python
import functools

import jax
import jax.numpy as jnp
from jax import lax
from jax.experimental import pallas as pl
from jax.experimental.pallas import tpu as pltpu
from jax.sharding import PartitionSpec as P

TIME_STEP = 0.1
SECTION_SHIFT = 2.0 / 3.0
FIRST_WEIGHT = 0.25
SECOND_WEIGHT = 0.75
MID = TIME_STEP * SECTION_SHIFT
W1 = TIME_STEP * FIRST_WEIGHT
W2 = TIME_STEP * SECOND_WEIGHT
CHUNKS = 2
SHARES = (1,)
COST_SHARE = 0.01
GROUP = 4
WIDE = 56 * 1024 * 1024

F32 = jnp.float32
BF16 = jnp.bfloat16
VMEM = pl.BlockSpec(memory_space=pltpu.VMEM)
SMEM = pl.BlockSpec(memory_space=pltpu.SMEM)
HBM = pl.BlockSpec(memory_space=pltpu.HBM)
EXTRA = 16
LIMIT = 16 * 1024 * 1024


def params(limit=LIMIT):
    return pltpu.CompilerParams(vmem_limit_bytes=limit)


def cost(flops, nbytes, trans=0):
    return pl.CostEstimate(
        flops=int(flops * COST_SHARE), bytes_accessed=int(nbytes * COST_SHARE), transcendentals=int(trans * COST_SHARE)
    )


def struct(shape, dtype):
    return jax.ShapeDtypeStruct(shape, dtype)


def build_kernel(first, count, near_cols, far_cols, far_ranks, near_in, left_in, right_in, out, *scratch):
    near, left, right, spread, dense, held, sems, out_sems = scratch
    slots, cell = near.shape[2], near.shape[3]
    far_slots, rank = left.shape[2], left.shape[3]
    pairs = ((near_in, near), (left_in, left), (right_in, right))
    copies, stores = [], []
    for i in range(0, count, GROUP):
        copies.append(
            [
                pltpu.make_async_copy(src.at[pl.ds(first + i, GROUP)], dst.at[pl.ds(i, GROUP)], sems.at[n, i // GROUP])
                for n, (src, dst) in enumerate(pairs)
            ]
        )
        at = pl.ds(i * cell, GROUP * cell)
        stores.append(pltpu.make_async_copy(held.at[at], out.at[at], out_sems.at[i // GROUP]))
    for group in copies:
        for copy in group:
            copy.start()
    ranks = lax.broadcasted_iota(jnp.int32, (rank, cell), 0)
    spread[...] = jnp.zeros_like(spread)
    dense[...] = jnp.zeros_like(dense)

    def far_place(q, k):
        return pl.ds(pl.multiple_of(far_cols[k, 0, q] * cell, cell), cell)

    def near_place(q, k):
        return pl.ds(pl.multiple_of(jnp.maximum(near_cols[k, 0, q], 0) * cell, cell), cell)

    for i in range(count):
        q = first + i
        turn = i % 2
        if i % GROUP == 0:
            for copy in copies[i // GROUP]:
                copy.wait()
        if i >= 2:
            for k in range(far_slots):
                spread[turn, pl.ds(k * rank, rank), far_place(q - 2, k)] = jnp.zeros((rank, cell), BF16)
            for k in range(slots):
                dense[turn, :, near_place(q - 2, k)] = jnp.zeros((cell, cell), BF16)
        for k in range(far_slots):
            kept = jnp.where(ranks < far_ranks[k, 0, q], right[i, 0, k], jnp.zeros((), BF16))
            spread[turn, pl.ds(k * rank, rank), far_place(q, k)] = kept
        for k in range(slots):

            @pl.when(near_cols[k, 0, q] >= 0)
            def _():
                dense[turn, :, near_place(q, k)] = near[i, 0, k]

        product = lax.dot_general(
            left[i, 0].reshape(far_slots * rank, cell),
            spread[turn],
            (((0,), (0,)), ((), ())),
            preferred_element_type=F32,
        )
        held[pl.ds(i * cell, cell)] = (product + dense[turn].astype(F32)).astype(BF16)
        if i % GROUP == GROUP - 1:
            stores[i // GROUP].start()
    for store in stores:
        store.wait()


def build_matrix(tables, factors, width, first, count):
    near, left, right = factors
    cell = near.shape[3]
    far_slots, rank = left.shape[2:4]
    depth = width * cell
    held = [pltpu.VMEM((count,) + array.shape[1:], BF16) for array in factors]
    return pl.pallas_call(
        functools.partial(build_kernel, first, count),
        out_shape=struct((count * cell, depth), BF16),
        in_specs=[SMEM] * 3 + [HBM] * 3,
        out_specs=HBM,
        scratch_shapes=held
        + [
            pltpu.VMEM((2, far_slots * rank, depth), BF16),
            pltpu.VMEM((2, cell, depth), BF16),
            pltpu.VMEM((count * cell, depth), BF16),
            pltpu.SemaphoreType.DMA((3, count // GROUP)),
            pltpu.SemaphoreType.DMA((count // GROUP,)),
        ],
        compiler_params=params(WIDE),
        cost_estimate=cost(2 * count * cell * far_slots * rank * depth, 2 * (near.size + left.size + right.size)),
        name="build_matrix",
    )(*tables, *factors)


def copy_picked(sel, sources, out, cell):
    pair_patches = sel.shape[0]
    for t in range(pair_patches):
        which = lax.div(sel[t], pair_patches)
        block = pl.multiple_of(lax.rem(sel[t], pair_patches) * cell, cell)
        for m, source in enumerate(sources):

            @pl.when(which == m)
            def _():
                out[pl.ds(t * cell, cell)] = source[pl.ds(block, cell)]


def pick_kernel(cell, sel, *refs):
    copy_picked(sel, refs[:-1], refs[-1], cell)


def pick(sel, sources, cell):
    return pl.pallas_call(
        functools.partial(pick_kernel, cell),
        out_shape=struct(sources[0].shape, BF16),
        in_specs=[SMEM] + [VMEM] * len(sources),
        out_specs=VMEM,
        compiler_params=params(),
        cost_estimate=cost(0, 4 * sources[0].size),
        name="pick",
    )(sel, *sources)


def read_extra(ref, count):
    high = ref.shape[0] - EXTRA
    tile = ref[pl.ds(high, EXTRA), pl.ds(0, 128)].astype(F32)
    return [jnp.max(tile[i : i + 1]).astype(jnp.int32) for i in range(count)]


def write_extra(ref, values):
    high, lanes = ref.shape[0] - EXTRA, ref.shape[1]
    at = lax.broadcasted_iota(jnp.int32, (EXTRA, lanes), 0)
    tile = jnp.zeros((EXTRA, lanes), F32)
    for i, value in values:
        tile = jnp.where(at == i, value.astype(F32), tile)
    ref[pl.ds(high, EXTRA)] = tile.astype(BF16)


def first_pick_kernel(cell, width, patch_count, perm, *refs):
    sources, (out, sel, rows, inv, ids) = refs[:-5], refs[-5:]
    pair_patches = 2 * patch_count
    for m, source in enumerate(sources):
        for i, q in enumerate(read_extra(source, pair_patches)):
            inv[q] = m * pair_patches + i
            rows[m * pair_patches + i] = q
    col = lax.axis_index("col")
    for n, group in enumerate((col, col + 1 - 2 * lax.rem(col, 2))):

        def choose(q, count, n=n, group=group):
            hit = lax.div(perm[q], width) == group

            @pl.when(hit)
            def _():
                sel[n * patch_count + count] = inv[q]
                ids[n * patch_count + count] = lax.rem(perm[q], width)

            return count + hit.astype(jnp.int32)

        lax.fori_loop(0, perm.shape[0], choose, jnp.int32(0))
    copy_picked(sel, sources, out, cell)
    write_extra(out, [(t, ids[t]) for t in range(pair_patches)])


def first_pick(perm, sources, cell, width, patch_count):
    rows_dev = perm.shape[0]
    return pl.pallas_call(
        functools.partial(first_pick_kernel, cell, width, patch_count),
        out_shape=(
            struct(sources[0].shape, BF16),
            struct((2 * patch_count,), jnp.int32),
            struct((rows_dev,), jnp.int32),
        ),
        in_specs=[SMEM] + [VMEM] * len(sources),
        out_specs=(VMEM, SMEM, SMEM),
        scratch_shapes=[pltpu.SMEM((rows_dev,), jnp.int32), pltpu.SMEM((2 * patch_count,), jnp.int32)],
        compiler_params=params(),
        cost_estimate=cost(1000, 4 * sources[0].size),
        name="first_pick",
    )(perm, *sources)


def apply_kernel(n_part, n_pair, n_row, cell, patch_count, first, *refs):
    m_own, m_sib = refs[:n_part], refs[n_part : 2 * n_part]
    pieces = refs[2 * n_part : 2 * n_part + n_row]
    rows, refs = refs[2 * n_part + n_row], refs[2 * n_part + n_row + 1 :]
    pair_patches = 2 * patch_count
    if not first:
        ids, refs = refs[0], refs[1:]
    outs, refs = refs[:n_pair], refs[n_pair:]
    if first:
        ids, refs = refs[0], refs[1:]
        for s in range(n_row):
            for t, block in enumerate(read_extra(pieces[s], pair_patches)):
                ids[s * pair_patches + t] = block
    x_own, x_sib, total = refs
    for s in range(n_row):
        for t in range(pair_patches):
            at = pl.ds(pl.multiple_of(ids[s * pair_patches + t] * cell, cell), cell)
            (x_own if t < patch_count else x_sib)[at] = pieces[s][pl.ds(t * cell, cell)]
    high, base = pair_patches * cell, 0
    for own, sib in zip(m_own, m_sib):
        for at in range(0, own.shape[0], high):
            part = jnp.dot(own[pl.ds(at, high)], x_own[...], preferred_element_type=F32)
            part = part + jnp.dot(sib[pl.ds(at, high)], x_sib[...], preferred_element_type=F32)
            total[pl.ds(base + at, high)] = part
        base += own.shape[0]
    for m in range(n_pair):
        for i in range(pair_patches):
            at = pl.ds(pl.multiple_of(rows[m * pair_patches + i] * cell, cell), cell)
            outs[m][pl.ds(i * cell, cell)] = total[at].astype(outs[m].dtype)


def apply_matrix(m_own, m_sib, pieces, rows, ids, cell, patch_count):
    n_row, n_part = len(pieces), len(m_own)
    high, depth = 2 * patch_count * cell, m_own[0].shape[1]
    rows_dev = rows.shape[0]
    n_pair = rows_dev * cell // high
    lanes = pieces[0].shape[1]
    first = ids is None
    extra = [] if first else [ids]
    ids_shape = struct((n_row * 2 * patch_count,), jnp.int32)
    return pl.pallas_call(
        functools.partial(apply_kernel, n_part, n_pair, n_row, cell, patch_count, first),
        out_shape=tuple(struct((high, lanes), F32 if m == 0 else BF16) for m in range(n_pair))
        + ((ids_shape,) if first else ()),
        in_specs=[VMEM] * (2 * n_part + n_row) + [SMEM] * (1 + len(extra)),
        out_specs=(VMEM,) * n_pair + ((SMEM,) if first else ()),
        scratch_shapes=[pltpu.VMEM((depth, lanes), BF16)] * 2 + [pltpu.VMEM((rows_dev * cell, lanes), F32)],
        compiler_params=params(48 * 1024 * 1024 if n_pair > 4 else LIMIT),
        cost_estimate=cost(4 * n_pair * high * depth * lanes, 4 * n_pair * high * depth),
        name="apply_matrix",
    )(*m_own, *m_sib, *pieces, rows, *extra)


def start_kernel(chunks, patch_rows, stress_in, state_in, direct_in, *refs):
    keep, give = refs[:chunks], refs[chunks : 2 * chunks]
    stress, state, direct, sems = refs[2 * chunks :]
    pairs = ((stress_in, stress), (state_in, state), (direct_in, direct))
    tile = stress.shape[0] // GROUP
    copies = [
        [
            pltpu.make_async_copy(src.at[pl.ds(g * tile, tile)], dst.at[pl.ds(g * tile, tile)], sems.at[n, g])
            for n, (src, dst) in enumerate(pairs)
        ]
        for g in range(GROUP)
    ]
    for group in copies:
        for copy in group:
            copy.start()
    half = stress.shape[1] // 2
    lanes = half // chunks
    patch_count = patch_rows.shape[0]
    side = lax.rem(lax.axis_index("col"), 2)
    for ref in (keep[0], give[0]):
        write_extra(ref, [(side * patch_count + i, patch_rows[i]) for i in range(patch_count)])
    for g, group in enumerate(copies):
        for copy in group:
            copy.wait()
        down = pl.ds(g * tile, tile)
        for own, outs in ((False, give), (True, keep)):
            base = (side if own else 1 - side) * half
            for j in range(chunks):
                at = pl.ds(pl.multiple_of(base + j * lanes, lanes), lanes)
                inverse = 1.0 / direct[down, at]
                stress_now, state_now = stress[down, at], state[down, at]
                velocity = jnp.exp((stress_now - state_now) * inverse) - jnp.exp((-stress_now - state_now) * inverse)
                outs[j][down] = velocity.astype(BF16)


def start(patch_rows, stress, state, direct, chunks):
    high, members = stress.shape
    lanes = members // 2 // chunks
    shapes = tuple(struct((high + (EXTRA if j == 0 else 0), lanes), BF16) for j in range(chunks))
    return pl.pallas_call(
        functools.partial(start_kernel, chunks),
        out_shape=shapes * 2,
        in_specs=[SMEM] + [HBM] * 3,
        out_specs=(VMEM,) * (2 * chunks),
        scratch_shapes=[pltpu.VMEM(stress.shape, F32)] * 3 + [pltpu.SemaphoreType.DMA((3, GROUP))],
        compiler_params=params(WIDE),
        cost_estimate=cost(10 * stress.size, 14 * stress.size, 3 * stress.size),
        name="start",
    )(patch_rows, stress, state, direct)


def mid_kernel(chunks, stress, state, direct, evolve, relax, load, keep, give, base, state_base):
    half = stress.shape[1] // 2
    lanes = half // chunks
    side = lax.rem(lax.axis_index("col"), 2)
    for own, ref in ((True, keep), (False, give)):
        first = (side if own else 1 - side) * half
        for j in range(chunks):
            at = pl.ds(pl.multiple_of(first + j * lanes, lanes), lanes)
            inverse = 1.0 / direct[:, at]
            inverse_e = 1.0 / evolve[:, at]
            stress_now, state_now = stress[:, at], state[:, at]
            relax_now, load_now = relax[:, at], load[:, at]
            velocity = jnp.exp((stress_now - state_now) * inverse) - jnp.exp((-stress_now - state_now) * inverse)
            state_rate = relax_now * (jnp.exp(-state_now * inverse_e) - velocity)
            state_mid = state_now + MID * state_rate
            ref[j, 0] = stress_now + MID * load_now
            ref[j, 1] = inverse
            ref[j, 2] = jnp.exp(-state_mid * inverse)
            base[:, at] = stress_now + TIME_STEP * load_now
            state_base[:, at] = state_now + W1 * state_rate + W2 * relax_now * jnp.exp(-state_mid * inverse_e)


def mid(stress, state, direct, evolve, relax, load, chunks):
    high, members = stress.shape
    lanes = members // 2 // chunks
    tile = 128
    wide = pl.BlockSpec((tile, members), lambda i: (i, 0))
    split = pl.BlockSpec((chunks, 3, tile, lanes), lambda i: (0, 0, i, 0))
    return pl.pallas_call(
        functools.partial(mid_kernel, chunks),
        out_shape=(struct((chunks, 3, high, lanes), F32),) * 2 + (struct(stress.shape, F32),) * 2,
        grid=(high // tile,),
        in_specs=[wide] * 6,
        out_specs=(split, split, wide, wide),
        compiler_params=params(),
        cost_estimate=cost(20 * stress.size, 44 * stress.size, 6 * stress.size),
        name="mid",
    )(stress, state, direct, evolve, relax, load)


def merge_kernel(high, keep, recv, out):
    side = lax.rem(lax.axis_index("col"), 2)
    out[pl.ds(pl.multiple_of(side * high, high), high)] = keep[pl.ds(0, high)]
    out[pl.ds(pl.multiple_of((1 - side) * high, high), high)] = recv[pl.ds(0, high)]
    if keep.shape[0] > high:
        out[pl.ds(2 * high, EXTRA)] = keep[pl.ds(high, EXTRA)] + recv[pl.ds(high, EXTRA)]


def merge(keep, recv, high):
    return pl.pallas_call(
        functools.partial(merge_kernel, high),
        out_shape=struct((keep.shape[0] + high, keep.shape[1]), keep.dtype),
        in_specs=[VMEM, VMEM],
        out_specs=VMEM,
        compiler_params=params(),
        cost_estimate=cost(0, 8 * keep.size),
        name="merge",
    )(keep, recv)


def second_kernel(keep, recv, *refs):
    n_pair = len(refs) - 4
    parts = refs[:n_pair]
    total_out, vel_b, vel_keep, vel_give = refs[n_pair:]
    high = keep.shape[2]
    side = lax.rem(lax.axis_index("col"), 2)
    for own, held, vel_out in ((True, keep, vel_keep), (False, recv, vel_give)):
        at = pl.ds(pl.multiple_of((side if own else 1 - side) * high, high), high)
        total = parts[0][at]
        for m in range(1, n_pair):
            total = total + parts[m][at].astype(F32)
        total_out[at] = W1 * total
        scaled = (held[0, 0] - MID * total) * held[0, 1]
        velocity = held[0, 2] * (jnp.exp(scaled) - jnp.exp(-scaled))
        vel_b[at] = velocity.astype(BF16)
        vel_out[...] = velocity


def second(keep, recv, parts, chunk):
    high, lanes = parts[0].shape
    held = pl.BlockSpec((1, 3, high // 2, lanes), lambda i: (chunk, 0, 0, 0))
    whole = pl.BlockSpec((high, lanes), lambda i: (0, 0))
    half = pl.BlockSpec((high // 2, lanes), lambda i: (0, 0))
    return pl.pallas_call(
        second_kernel,
        out_shape=(struct((high, lanes), F32), struct((high, lanes), BF16))
        + (struct((high // 2, lanes), F32),) * 2,
        grid=(1,),
        in_specs=[held, held] + [whole] * len(parts),
        out_specs=(whole, whole, half, half),
        compiler_params=params(),
        cost_estimate=cost(10 * high * lanes, 40 * high * lanes, 2 * high * lanes),
        name="second",
    )(keep, recv, *parts)


def weigh_kernel(first, *refs):
    parts = refs[:-2]
    keep, give = refs[-2:]
    high = keep.shape[0]
    side = lax.rem(lax.axis_index("col"), 2)
    for own, ref in ((False, give), (True, keep)):
        at = pl.ds(pl.multiple_of((side if own else 1 - side) * high, high), high)
        total = parts[0][at]
        for part in parts[1:]:
            total = total + part[at].astype(F32)
        ref[...] = first[at] + W2 * total


def weigh(first, parts):
    high, lanes = first.shape
    return pl.pallas_call(
        weigh_kernel,
        out_shape=(struct((high // 2, lanes), F32),) * 2,
        in_specs=[VMEM] * (1 + len(parts)),
        out_specs=(VMEM, VMEM),
        compiler_params=params(),
        cost_estimate=cost(10 * high * lanes, 20 * high * lanes),
        name="weigh",
    )(first, *parts)


def finish_kernel(chunks, scaled, base, *refs):
    out = refs[-1]
    factor = refs[0] if scaled else None
    pieces = refs[1:-1] if scaled else refs[:-1]
    half = base.shape[1] // 2
    lanes = half // chunks
    side = lax.rem(lax.axis_index("col"), 2)
    for j in range(chunks):
        for own, piece in ((True, pieces[j]), (False, pieces[chunks + j])):
            first = (side if own else 1 - side) * half + j * lanes
            at = pl.ds(pl.multiple_of(first, lanes), lanes)
            change = piece[...]
            if scaled:
                change = W2 * factor[:, at] * change
            out[:, at] = base[:, at] - change


def finish(base, factor, keeps, recvs):
    chunks = len(keeps)
    scaled = factor is not None
    extra = [factor] if scaled else []
    return pl.pallas_call(
        functools.partial(finish_kernel, chunks, scaled),
        out_shape=struct(base.shape, F32),
        in_specs=[VMEM] * (1 + len(extra) + 2 * chunks),
        out_specs=VMEM,
        compiler_params=params(),
        cost_estimate=cost(3 * base.size, 16 * base.size),
        name="finish",
    )(base, *extra, *keeps, *recvs)


def shards(
    stress,
    friction_state,
    direct,
    evolve,
    relax_rate,
    load_rate,
    row_perm,
    patch_rows,
    near_cols,
    near_blocks,
    far_cols,
    far_ranks,
    far_left,
    far_right,
):
    n_col, n_row = lax.axis_size("col"), lax.axis_size("row")
    n_pair = n_col // 2
    rows_dev = row_perm.shape[0]
    patch_count = patch_rows.shape[0]
    width = rows_dev * n_row // n_col
    cell = near_blocks.shape[-1]

    def after(values, dep):
        return lax.optimization_barrier((values, dep))[0]

    def swap(x):
        return lax.ppermute(x, "col", [(i, i ^ 1) for i in range(n_col)])

    def across(x, m):
        return lax.ppermute(x, "col", [(i, i ^ (2 * m)) for i in range(n_col)])

    def along(x, s):
        return lax.ppermute(x, "row", [(i, i ^ s) for i in range(n_row)])

    def after(values, dep):
        return lax.optimization_barrier((values, dep))[0]

    high = stress.shape[0]
    started = start(patch_rows, stress, friction_state, direct, CHUNKS)
    keep_first, give_first = started[:CHUNKS], started[CHUNKS:]
    tables = after([t.transpose(2, 1, 0) for t in (near_cols, far_cols, far_ranks)], give_first[0])
    factors = (near_blocks, far_left, far_right)
    unit = rows_dev // sum(SHARES)
    m_own, first_row = [], 0
    for share in SHARES:
        m_own.append(build_matrix(tables, factors, width, first_row, share * unit))
        first_row += share * unit
    recv_first = [swap(give) for give in give_first]
    held = (stress, friction_state, direct, evolve, relax_rate, load_rate)
    keep_mid, give_mid, base, state_base = mid(*after(held, m_own), CHUNKS)
    recv_first, m_own, give_mid = lax.optimization_barrier((recv_first, m_own, give_mid))
    m_sib = [swap(m) for m in m_own]
    recv_mid = swap(give_mid)

    def spread(vel_b):
        return [vel_b] + [across(vel_b, m) for m in range(1, n_pair)]

    def gather(chosen, dep=None):
        pieces, step = [chosen], n_row // 2
        while step:
            sent = [along(piece, step) for piece in pieces]
            if dep is not None:
                sent, dep = after(sent, dep), None
            pieces = pieces + sent
            step //= 2
        return pieces

    def reduce(partial):
        return [partial[0]] + [across(partial[m], m) for m in range(1, n_pair)]

    n = CHUNKS
    sources = spread(merge(keep_first[0], recv_first[0], high))
    perm = after(row_perm, (m_sib, recv_mid))
    chosen, sel, rows = first_pick(perm, sources, cell, width, patch_count)
    picked, arrived, partials, ids, dep = [chosen], [], [], None, chosen
    for j in range(1, n):
        sources = spread(merge(keep_first[j], after(recv_first[j], dep), high))
        arrived.append(gather(picked[-1], sources[1:]))
        partials.append(apply_matrix(m_own, m_sib, arrived[-1], rows, ids, cell, patch_count))
        ids = partials[-1][-1] if ids is None else ids
        picked.append(pick(after(sel, partials[-1][0]), sources, cell))
        dep = picked[-1]
    arrived.append(gather(picked[-1]))
    firsts, vel_keeps, vel_recvs, keeps, recvs = [], [], [], [], []
    dep, held_vel, last = None, [], []
    for j in range(n):
        if j == n - 1:
            rows_j = rows if dep is None else after(rows, dep)
            partials.append(apply_matrix(m_own, m_sib, arrived[j], rows_j, ids, cell, patch_count))
            ids = partials[-1][-1] if ids is None else ids
        parts = reduce(partials[j])
        if held_vel:
            parts[0] = after(parts[0], held_vel[-1])
        first, vel_b, vel_keep, vel_give = second(keep_mid, recv_mid, parts, j)
        dep = vel_b
        firsts.append(first)
        vel_keeps.append(vel_keep)
        vel_recvs.append(swap(vel_give))
        sel_j = sel if j == 0 else after(sel, last[-1][0])
        held_vel.append(pick(sel_j, spread(vel_b), cell))
        arrived.append(gather(held_vel[-1]))
        if j < n - 1:
            last.append(apply_matrix(m_own, m_sib, arrived[-1], rows, ids, cell, patch_count))
    for j in range(n):
        if j == n - 1:
            rows_j = rows if j == 0 else after(rows, keeps[-1])
            last.append(apply_matrix(m_own, m_sib, arrived[-1], rows_j, ids, cell, patch_count))
        keep, give = weigh(firsts[j], reduce(last[j]))
        keeps.append(keep)
        recvs.append(swap(give))
    state_next = finish(state_base, relax_rate, vel_keeps, vel_recvs)
    stress_next = finish(base, None, keeps, recvs)
    return (stress_next, state_next)


def solution(mesh):
    cells = P(("row", "col"), None)
    placed = (
        cells,
        cells,
        cells,
        cells,
        cells,
        cells,
        P("row"),
        P(("row", "col")),
        P("row", "col", None),
        P("row", "col", None, None, None),
        P("row", "col", None),
        P("row", "col", None),
        P("row", "col", None, None, None),
        P("row", "col", None, None, None),
    )
    return jax.shard_map(
        shards,
        mesh=mesh,
        in_specs=placed,
        out_specs=(cells, cells),
        check_vma=False,
    )
```

```python
import functools

import jax
import jax.numpy as jnp
from jax import lax
from jax.experimental import pallas as pl
from jax.experimental.pallas import tpu as pltpu
from jax.sharding import PartitionSpec as P

TIME_STEP = 0.1
SECTION_SHIFT = 2.0 / 3.0
FIRST_WEIGHT = 0.25
SECOND_WEIGHT = 0.75
MID = TIME_STEP * SECTION_SHIFT
W1 = TIME_STEP * FIRST_WEIGHT
W2 = TIME_STEP * SECOND_WEIGHT
CHUNKS = 2
SHARES = (1,)
COST_SHARE = 0.01
GROUP = 4
WIDE = 56 * 1024 * 1024

F32 = jnp.float32
BF16 = jnp.bfloat16
VMEM = pl.BlockSpec(memory_space=pltpu.VMEM)
SMEM = pl.BlockSpec(memory_space=pltpu.SMEM)
HBM = pl.BlockSpec(memory_space=pltpu.HBM)
EXTRA = 16
LIMIT = 16 * 1024 * 1024


def params(limit=LIMIT):
    return pltpu.CompilerParams(vmem_limit_bytes=limit)


def cost(flops, nbytes, trans=0):
    return pl.CostEstimate(
        flops=int(flops * COST_SHARE), bytes_accessed=int(nbytes * COST_SHARE), transcendentals=int(trans * COST_SHARE)
    )


def struct(shape, dtype):
    return jax.ShapeDtypeStruct(shape, dtype)


def build_kernel(first, count, near_cols, far_cols, far_ranks, near_in, left_in, right_in, out, *scratch):
    near, left, right, spread, dense, held, sems, out_sems = scratch
    slots, cell = near.shape[2], near.shape[3]
    far_slots, rank = left.shape[2], left.shape[3]
    pairs = ((near_in, near), (left_in, left), (right_in, right))
    copies, stores = [], []
    for i in range(0, count, GROUP):
        copies.append(
            [
                pltpu.make_async_copy(src.at[pl.ds(first + i, GROUP)], dst.at[pl.ds(i, GROUP)], sems.at[n, i // GROUP])
                for n, (src, dst) in enumerate(pairs)
            ]
        )
        at = pl.ds(i * cell, GROUP * cell)
        stores.append(pltpu.make_async_copy(held.at[at], out.at[at], out_sems.at[i // GROUP]))
    for group in copies:
        for copy in group:
            copy.start()
    ranks = lax.broadcasted_iota(jnp.int32, (rank, cell), 0)
    spread[...] = jnp.zeros_like(spread)
    dense[...] = jnp.zeros_like(dense)

    def far_place(q, k):
        return pl.ds(pl.multiple_of(far_cols[k, 0, q] * cell, cell), cell)

    def near_place(q, k):
        return pl.ds(pl.multiple_of(jnp.maximum(near_cols[k, 0, q], 0) * cell, cell), cell)

    for i in range(count):
        q = first + i
        turn = i % 2
        if i % GROUP == 0:
            for copy in copies[i // GROUP]:
                copy.wait()
        if i >= 2:
            for k in range(far_slots):
                spread[turn, pl.ds(k * rank, rank), far_place(q - 2, k)] = jnp.zeros((rank, cell), BF16)
            for k in range(slots):
                dense[turn, :, near_place(q - 2, k)] = jnp.zeros((cell, cell), BF16)
        for k in range(far_slots):
            kept = jnp.where(ranks < far_ranks[k, 0, q], right[i, 0, k], jnp.zeros((), BF16))
            spread[turn, pl.ds(k * rank, rank), far_place(q, k)] = kept
        for k in range(slots):

            @pl.when(near_cols[k, 0, q] >= 0)
            def _():
                dense[turn, :, near_place(q, k)] = near[i, 0, k]

        product = lax.dot_general(
            left[i, 0].reshape(far_slots * rank, cell),
            spread[turn],
            (((0,), (0,)), ((), ())),
            preferred_element_type=F32,
        )
        held[pl.ds(i * cell, cell)] = (product + dense[turn].astype(F32)).astype(BF16)
        if i % GROUP == GROUP - 1:
            stores[i // GROUP].start()
    for store in stores:
        store.wait()


def build_matrix(tables, factors, width, first, count):
    near, left, right = factors
    cell = near.shape[3]
    far_slots, rank = left.shape[2:4]
    depth = width * cell
    held = [pltpu.VMEM((count,) + array.shape[1:], BF16) for array in factors]
    return pl.pallas_call(
        functools.partial(build_kernel, first, count),
        out_shape=struct((count * cell, depth), BF16),
        in_specs=[SMEM] * 3 + [HBM] * 3,
        out_specs=HBM,
        scratch_shapes=held
        + [
            pltpu.VMEM((2, far_slots * rank, depth), BF16),
            pltpu.VMEM((2, cell, depth), BF16),
            pltpu.VMEM((count * cell, depth), BF16),
            pltpu.SemaphoreType.DMA((3, count // GROUP)),
            pltpu.SemaphoreType.DMA((count // GROUP,)),
        ],
        compiler_params=params(WIDE),
        cost_estimate=cost(2 * count * cell * far_slots * rank * depth, 2 * (near.size + left.size + right.size)),
        name="build_matrix",
    )(*tables, *factors)


def copy_picked(sel, sources, out, cell):
    pair_patches = sel.shape[0]
    for t in range(pair_patches):
        which = lax.div(sel[t], pair_patches)
        block = pl.multiple_of(lax.rem(sel[t], pair_patches) * cell, cell)
        for m, source in enumerate(sources):

            @pl.when(which == m)
            def _():
                out[pl.ds(t * cell, cell)] = source[pl.ds(block, cell)]


def pick_kernel(cell, sel, *refs):
    copy_picked(sel, refs[:-1], refs[-1], cell)


def pick(sel, sources, cell):
    return pl.pallas_call(
        functools.partial(pick_kernel, cell),
        out_shape=struct(sources[0].shape, BF16),
        in_specs=[SMEM] + [VMEM] * len(sources),
        out_specs=VMEM,
        compiler_params=params(),
        cost_estimate=cost(0, 4 * sources[0].size),
        name="pick",
    )(sel, *sources)


def read_extra(ref, count):
    high = ref.shape[0] - EXTRA
    tile = ref[pl.ds(high, EXTRA), pl.ds(0, 128)].astype(F32)
    return [jnp.max(tile[i : i + 1]).astype(jnp.int32) for i in range(count)]


def write_extra(ref, values):
    high, lanes = ref.shape[0] - EXTRA, ref.shape[1]
    at = lax.broadcasted_iota(jnp.int32, (EXTRA, lanes), 0)
    tile = jnp.zeros((EXTRA, lanes), F32)
    for i, value in values:
        tile = jnp.where(at == i, value.astype(F32), tile)
    ref[pl.ds(high, EXTRA)] = tile.astype(BF16)


def first_pick_kernel(cell, width, patch_count, perm, *refs):
    sources, (out, sel, rows, inv, ids) = refs[:-5], refs[-5:]
    pair_patches = 2 * patch_count
    for m, source in enumerate(sources):
        for i, q in enumerate(read_extra(source, pair_patches)):
            inv[q] = m * pair_patches + i
            rows[m * pair_patches + i] = q
    col = lax.axis_index("col")
    for n, group in enumerate((col, col + 1 - 2 * lax.rem(col, 2))):

        def choose(q, count, n=n, group=group):
            hit = lax.div(perm[q], width) == group

            @pl.when(hit)
            def _():
                sel[n * patch_count + count] = inv[q]
                ids[n * patch_count + count] = lax.rem(perm[q], width)

            return count + hit.astype(jnp.int32)

        lax.fori_loop(0, perm.shape[0], choose, jnp.int32(0))
    copy_picked(sel, sources, out, cell)
    write_extra(out, [(t, ids[t]) for t in range(pair_patches)])


def first_pick(perm, sources, cell, width, patch_count):
    rows_dev = perm.shape[0]
    return pl.pallas_call(
        functools.partial(first_pick_kernel, cell, width, patch_count),
        out_shape=(
            struct(sources[0].shape, BF16),
            struct((2 * patch_count,), jnp.int32),
            struct((rows_dev,), jnp.int32),
        ),
        in_specs=[SMEM] + [VMEM] * len(sources),
        out_specs=(VMEM, SMEM, SMEM),
        scratch_shapes=[pltpu.SMEM((rows_dev,), jnp.int32), pltpu.SMEM((2 * patch_count,), jnp.int32)],
        compiler_params=params(),
        cost_estimate=cost(1000, 4 * sources[0].size),
        name="first_pick",
    )(perm, *sources)


def apply_kernel(n_part, n_pair, n_row, cell, patch_count, first, *refs):
    m_own, m_sib = refs[:n_part], refs[n_part : 2 * n_part]
    pieces = refs[2 * n_part : 2 * n_part + n_row]
    rows, refs = refs[2 * n_part + n_row], refs[2 * n_part + n_row + 1 :]
    pair_patches = 2 * patch_count
    if not first:
        ids, refs = refs[0], refs[1:]
    outs, refs = refs[:n_pair], refs[n_pair:]
    if first:
        ids, refs = refs[0], refs[1:]
        for s in range(n_row):
            for t, block in enumerate(read_extra(pieces[s], pair_patches)):
                ids[s * pair_patches + t] = block
    x_own, x_sib, total = refs
    for s in range(n_row):
        for t in range(pair_patches):
            at = pl.ds(pl.multiple_of(ids[s * pair_patches + t] * cell, cell), cell)
            (x_own if t < patch_count else x_sib)[at] = pieces[s][pl.ds(t * cell, cell)]
    high, base = pair_patches * cell, 0
    for own, sib in zip(m_own, m_sib):
        for at in range(0, own.shape[0], high):
            part = jnp.dot(own[pl.ds(at, high)], x_own[...], preferred_element_type=F32)
            part = part + jnp.dot(sib[pl.ds(at, high)], x_sib[...], preferred_element_type=F32)
            total[pl.ds(base + at, high)] = part
        base += own.shape[0]
    for m in range(n_pair):
        for i in range(pair_patches):
            at = pl.ds(pl.multiple_of(rows[m * pair_patches + i] * cell, cell), cell)
            outs[m][pl.ds(i * cell, cell)] = total[at].astype(outs[m].dtype)


def apply_matrix(m_own, m_sib, pieces, rows, ids, cell, patch_count):
    n_row, n_part = len(pieces), len(m_own)
    high, depth = 2 * patch_count * cell, m_own[0].shape[1]
    rows_dev = rows.shape[0]
    n_pair = rows_dev * cell // high
    lanes = pieces[0].shape[1]
    first = ids is None
    extra = [] if first else [ids]
    ids_shape = struct((n_row * 2 * patch_count,), jnp.int32)
    return pl.pallas_call(
        functools.partial(apply_kernel, n_part, n_pair, n_row, cell, patch_count, first),
        out_shape=tuple(struct((high, lanes), F32 if m == 0 else BF16) for m in range(n_pair))
        + ((ids_shape,) if first else ()),
        in_specs=[VMEM] * (2 * n_part + n_row) + [SMEM] * (1 + len(extra)),
        out_specs=(VMEM,) * n_pair + ((SMEM,) if first else ()),
        scratch_shapes=[pltpu.VMEM((depth, lanes), BF16)] * 2 + [pltpu.VMEM((rows_dev * cell, lanes), F32)],
        compiler_params=params(48 * 1024 * 1024 if n_pair > 4 else LIMIT),
        cost_estimate=cost(4 * n_pair * high * depth * lanes, 4 * n_pair * high * depth),
        name="apply_matrix",
    )(*m_own, *m_sib, *pieces, rows, *extra)


def start_kernel(chunks, patch_rows, stress_in, state_in, direct_in, *refs):
    keep, give = refs[:chunks], refs[chunks : 2 * chunks]
    stress, state, direct, sems = refs[2 * chunks :]
    pairs = ((stress_in, stress), (state_in, state), (direct_in, direct))
    tile = stress.shape[0] // GROUP
    copies = [
        [
            pltpu.make_async_copy(src.at[pl.ds(g * tile, tile)], dst.at[pl.ds(g * tile, tile)], sems.at[n, g])
            for n, (src, dst) in enumerate(pairs)
        ]
        for g in range(GROUP)
    ]
    for group in copies:
        for copy in group:
            copy.start()
    half = stress.shape[1] // 2
    lanes = half // chunks
    patch_count = patch_rows.shape[0]
    side = lax.rem(lax.axis_index("col"), 2)
    for ref in (keep[0], give[0]):
        write_extra(ref, [(side * patch_count + i, patch_rows[i]) for i in range(patch_count)])
    for g, group in enumerate(copies):
        for copy in group:
            copy.wait()
        down = pl.ds(g * tile, tile)
        for own, outs in ((False, give), (True, keep)):
            base = (side if own else 1 - side) * half
            for j in range(chunks):
                at = pl.ds(pl.multiple_of(base + j * lanes, lanes), lanes)
                inverse = 1.0 / direct[down, at]
                stress_now, state_now = stress[down, at], state[down, at]
                velocity = jnp.exp((stress_now - state_now) * inverse) - jnp.exp((-stress_now - state_now) * inverse)
                outs[j][down] = velocity.astype(BF16)


def start(patch_rows, stress, state, direct, chunks):
    high, members = stress.shape
    lanes = members // 2 // chunks
    shapes = tuple(struct((high + (EXTRA if j == 0 else 0), lanes), BF16) for j in range(chunks))
    return pl.pallas_call(
        functools.partial(start_kernel, chunks),
        out_shape=shapes * 2,
        in_specs=[SMEM] + [HBM] * 3,
        out_specs=(VMEM,) * (2 * chunks),
        scratch_shapes=[pltpu.VMEM(stress.shape, F32)] * 3 + [pltpu.SemaphoreType.DMA((3, GROUP))],
        compiler_params=params(WIDE),
        cost_estimate=cost(10 * stress.size, 14 * stress.size, 3 * stress.size),
        name="start",
    )(patch_rows, stress, state, direct)


def mid_kernel(chunks, stress, state, direct, evolve, relax, load, keep, give, base, state_base):
    half = stress.shape[1] // 2
    lanes = half // chunks
    side = lax.rem(lax.axis_index("col"), 2)
    for own, ref in ((True, keep), (False, give)):
        first = (side if own else 1 - side) * half
        for j in range(chunks):
            at = pl.ds(pl.multiple_of(first + j * lanes, lanes), lanes)
            inverse = 1.0 / direct[:, at]
            inverse_e = 1.0 / evolve[:, at]
            stress_now, state_now = stress[:, at], state[:, at]
            relax_now, load_now = relax[:, at], load[:, at]
            velocity = jnp.exp((stress_now - state_now) * inverse) - jnp.exp((-stress_now - state_now) * inverse)
            state_rate = relax_now * (jnp.exp(-state_now * inverse_e) - velocity)
            state_mid = state_now + MID * state_rate
            ref[j, 0] = stress_now + MID * load_now
            ref[j, 1] = inverse
            ref[j, 2] = jnp.exp(-state_mid * inverse)
            base[:, at] = stress_now + TIME_STEP * load_now
            state_base[:, at] = state_now + W1 * state_rate + W2 * relax_now * jnp.exp(-state_mid * inverse_e)


def mid(stress, state, direct, evolve, relax, load, chunks):
    high, members = stress.shape
    lanes = members // 2 // chunks
    tile = 128
    wide = pl.BlockSpec((tile, members), lambda i: (i, 0))
    split = pl.BlockSpec((chunks, 3, tile, lanes), lambda i: (0, 0, i, 0))
    return pl.pallas_call(
        functools.partial(mid_kernel, chunks),
        out_shape=(struct((chunks, 3, high, lanes), F32),) * 2 + (struct(stress.shape, F32),) * 2,
        grid=(high // tile,),
        in_specs=[wide] * 6,
        out_specs=(split, split, wide, wide),
        compiler_params=params(),
        cost_estimate=cost(20 * stress.size, 44 * stress.size, 6 * stress.size),
        name="mid",
    )(stress, state, direct, evolve, relax, load)


def merge_kernel(high, keep, recv, out):
    side = lax.rem(lax.axis_index("col"), 2)
    out[pl.ds(pl.multiple_of(side * high, high), high)] = keep[pl.ds(0, high)]
    out[pl.ds(pl.multiple_of((1 - side) * high, high), high)] = recv[pl.ds(0, high)]
    if keep.shape[0] > high:
        out[pl.ds(2 * high, EXTRA)] = keep[pl.ds(high, EXTRA)] + recv[pl.ds(high, EXTRA)]


def merge(keep, recv, high):
    return pl.pallas_call(
        functools.partial(merge_kernel, high),
        out_shape=struct((keep.shape[0] + high, keep.shape[1]), keep.dtype),
        in_specs=[VMEM, VMEM],
        out_specs=VMEM,
        compiler_params=params(),
        cost_estimate=cost(0, 8 * keep.size),
        name="merge",
    )(keep, recv)


def second_kernel(keep, recv, *refs):
    n_pair = len(refs) - 4
    parts = refs[:n_pair]
    total_out, vel_b, vel_keep, vel_give = refs[n_pair:]
    high = keep.shape[2]
    side = lax.rem(lax.axis_index("col"), 2)
    for own, held, vel_out in ((True, keep, vel_keep), (False, recv, vel_give)):
        at = pl.ds(pl.multiple_of((side if own else 1 - side) * high, high), high)
        total = parts[0][at]
        for m in range(1, n_pair):
            total = total + parts[m][at].astype(F32)
        total_out[at] = W1 * total
        scaled = (held[0, 0] - MID * total) * held[0, 1]
        velocity = held[0, 2] * (jnp.exp(scaled) - jnp.exp(-scaled))
        vel_b[at] = velocity.astype(BF16)
        vel_out[...] = velocity


def second(keep, recv, parts, chunk):
    high, lanes = parts[0].shape
    held = pl.BlockSpec((1, 3, high // 2, lanes), lambda i: (chunk, 0, 0, 0))
    whole = pl.BlockSpec((high, lanes), lambda i: (0, 0))
    half = pl.BlockSpec((high // 2, lanes), lambda i: (0, 0))
    return pl.pallas_call(
        second_kernel,
        out_shape=(struct((high, lanes), F32), struct((high, lanes), BF16))
        + (struct((high // 2, lanes), F32),) * 2,
        grid=(1,),
        in_specs=[held, held] + [whole] * len(parts),
        out_specs=(whole, whole, half, half),
        compiler_params=params(),
        cost_estimate=cost(10 * high * lanes, 40 * high * lanes, 2 * high * lanes),
        name="second",
    )(keep, recv, *parts)


def weigh_kernel(first, *refs):
    parts = refs[:-2]
    keep, give = refs[-2:]
    high = keep.shape[0]
    side = lax.rem(lax.axis_index("col"), 2)
    for own, ref in ((False, give), (True, keep)):
        at = pl.ds(pl.multiple_of((side if own else 1 - side) * high, high), high)
        total = parts[0][at]
        for part in parts[1:]:
            total = total + part[at].astype(F32)
        ref[...] = first[at] + W2 * total


def weigh(first, parts):
    high, lanes = first.shape
    return pl.pallas_call(
        weigh_kernel,
        out_shape=(struct((high // 2, lanes), F32),) * 2,
        in_specs=[VMEM] * (1 + len(parts)),
        out_specs=(VMEM, VMEM),
        compiler_params=params(),
        cost_estimate=cost(10 * high * lanes, 20 * high * lanes),
        name="weigh",
    )(first, *parts)


def finish_kernel(chunks, scaled, base, *refs):
    out = refs[-1]
    factor = refs[0] if scaled else None
    pieces = refs[1:-1] if scaled else refs[:-1]
    half = base.shape[1] // 2
    lanes = half // chunks
    side = lax.rem(lax.axis_index("col"), 2)
    for j in range(chunks):
        for own, piece in ((True, pieces[j]), (False, pieces[chunks + j])):
            first = (side if own else 1 - side) * half + j * lanes
            at = pl.ds(pl.multiple_of(first, lanes), lanes)
            change = piece[...]
            if scaled:
                change = W2 * factor[:, at] * change
            out[:, at] = base[:, at] - change


def finish(base, factor, keeps, recvs):
    chunks = len(keeps)
    scaled = factor is not None
    extra = [factor] if scaled else []
    return pl.pallas_call(
        functools.partial(finish_kernel, chunks, scaled),
        out_shape=struct(base.shape, F32),
        in_specs=[VMEM] * (1 + len(extra) + 2 * chunks),
        out_specs=VMEM,
        compiler_params=params(),
        cost_estimate=cost(3 * base.size, 16 * base.size),
        name="finish",
    )(base, *extra, *keeps, *recvs)


def shards(
    stress,
    friction_state,
    direct,
    evolve,
    relax_rate,
    load_rate,
    row_perm,
    patch_rows,
    near_cols,
    near_blocks,
    far_cols,
    far_ranks,
    far_left,
    far_right,
):
    n_col, n_row = lax.axis_size("col"), lax.axis_size("row")
    n_pair = n_col // 2
    rows_dev = row_perm.shape[0]
    patch_count = patch_rows.shape[0]
    width = rows_dev * n_row // n_col
    cell = near_blocks.shape[-1]

    def after(values, dep):
        return lax.optimization_barrier((values, dep))[0]

    def swap(x):
        return lax.ppermute(x, "col", [(i, i ^ 1) for i in range(n_col)])

    def across(x, m):
        return lax.ppermute(x, "col", [(i, i ^ (2 * m)) for i in range(n_col)])

    def along(x, s):
        return lax.ppermute(x, "row", [(i, i ^ s) for i in range(n_row)])

    def after(values, dep):
        return lax.optimization_barrier((values, dep))[0]

    high = stress.shape[0]
    started = start(patch_rows, stress, friction_state, direct, CHUNKS)
    keep_first, give_first = started[:CHUNKS], started[CHUNKS:]
    recv_first = lax.optimization_barrier([swap(give) for give in give_first])
    vel_first = merge(keep_first[0], recv_first[0], high)
    tables = after([t.transpose(2, 1, 0) for t in (near_cols, far_cols, far_ranks)], vel_first)
    factors = (near_blocks, far_left, far_right)
    unit = rows_dev // sum(SHARES)
    m_own, first_row = [], 0
    for share in SHARES:
        m_own.append(build_matrix(tables, factors, width, first_row, share * unit))
        first_row += share * unit

    def spread(vel_b):
        return [vel_b] + [across(vel_b, m) for m in range(1, n_pair)]

    def gather(chosen, dep=None):
        pieces, step = [chosen], n_row // 2
        while step:
            sent = [along(pieces[0], step)]
            if dep is not None:
                sent, dep = after(sent, dep), None
            sent += [along(after(piece, sent[0]), step) for piece in pieces[1:]]
            pieces = pieces + sent
            step //= 2
        return pieces

    def gather_flat(chosen):
        order, step = [0], n_row // 2
        while step:
            order, step = order + [way ^ step for way in order], step // 2
        return [chosen] + [along(chosen, way) for way in order[1:]]

    def reduce(partial):
        return [partial[0]] + [across(partial[m], m) for m in range(1, n_pair)]

    n = CHUNKS
    sources = spread(vel_first)
    perm = after(row_perm, m_own)
    chosen, sel, rows = first_pick(perm, sources, cell, width, patch_count)
    m_sib = [swap(after(m, chosen)) for m in m_own]
    held = (stress, friction_state, direct, evolve, relax_rate, load_rate)
    keep_mid, give_mid, base, state_base = mid(*after(held, chosen), CHUNKS)
    recv_mid = swap(give_mid)
    picked, arrived, partials, ids, dep = [chosen], [], [], None, chosen
    for j in range(1, n):
        arrived.append(gather(picked[-1]))
        sources = spread(merge(keep_first[j], after(recv_first[j], arrived[-1][1]), high))
        partials.append(apply_matrix(m_own, m_sib, arrived[-1], rows, ids, cell, patch_count))
        ids = partials[-1][-1] if ids is None else ids
        picked.append(pick(after(sel, (partials[-1][0], recv_mid)), sources, cell))
        dep = picked[-1]
    arrived.append(gather(picked[-1]))
    firsts, vel_keeps, vel_recvs, keeps, recvs = [], [], [], [], []
    dep, held_vel, last = None, [], []
    for j in range(n):
        if j == n - 1:
            rows_j = rows if dep is None else after(rows, dep)
            partials.append(apply_matrix(m_own, m_sib, arrived[j], rows_j, ids, cell, patch_count))
            ids = partials[-1][-1] if ids is None else ids
        parts = reduce(partials[j])
        if held_vel:
            parts[0] = after(parts[0], held_vel[-1])
        first, vel_b, vel_keep, vel_give = second(keep_mid, recv_mid, parts, j)
        dep = vel_b
        firsts.append(first)
        vel_keeps.append(vel_keep)
        vel_recvs.append(swap(vel_give))
        sel_j = sel
        held_vel.append(pick(sel_j, spread(vel_b), cell))
        arrived.append((gather_flat if j == n - 1 else gather)(held_vel[-1]))
        if j < n - 1:
            last.append(apply_matrix(m_own, m_sib, arrived[-1], rows, ids, cell, patch_count))
    for j in range(n):
        if j == n - 1:
            rows_j = rows
            last.append(apply_matrix(m_own, m_sib, arrived[-1], rows_j, ids, cell, patch_count))
        keep, give = weigh(firsts[j], reduce(last[j]))
        keeps.append(keep)
        recvs.append(swap(give))
    state_next = finish(state_base, relax_rate, vel_keeps, vel_recvs)
    stress_next = finish(base, None, keeps, recvs)
    return (stress_next, state_next)


def solution(mesh):
    cells = P(("row", "col"), None)
    placed = (
        cells,
        cells,
        cells,
        cells,
        cells,
        cells,
        P("row"),
        P(("row", "col")),
        P("row", "col", None),
        P("row", "col", None, None, None),
        P("row", "col", None),
        P("row", "col", None),
        P("row", "col", None, None, None),
        P("row", "col", None, None, None),
    )
    return jax.shard_map(
        shards,
        mesh=mesh,
        in_specs=placed,
        out_specs=(cells, cells),
        check_vma=False,
    )
```
